32 devices in a mesh: grid: 16 (over z, y, core), batch: 2 (over x).
Axes of the slice: x: 2, y: 2, z: 4, core: 2. Of those that a mesh axis runs over, the one named last changes fastest.
Arguments:
- inputs: bfloat16 [2, 256, 16384], P('batch', None, 'grid'), may hold values from -6 to 6
- cotangent: bfloat16 [2, 256, 16384], P('batch', None, 'grid'), may hold values from -8 to 8
- weights: bfloat16 [128, 8, 9216], P('grid', 'batch'), may hold values from -0.375 to 0.375
- gate_logits: float32 [2, 64, 2], replicated, may hold values from -5 to 5
- routes: int32 [2, 64, 2], replicated, may hold values from 0 to 127, as said below
Outputs:
- d_inputs: bfloat16 [2, 256, 16384], P('batch', None, 'grid')
- d_weights: float32 [128, 8, 9216], P('grid', 'batch')
- gate_grad: float32 [2, 64, 2], P(None, 'grid')
The draws below stay inside these ranges and needn't reach their ends.
Inputs may be any that keep to these rules, and one draw needn't show every extreme that they name: Expert e is owned by grid index e // 8. The 16 routes of the patches g * 4 to (g + 1) * 4 - 1 of all samples name experts of one owner at most 1 times, for every grid index g; in every draw some owner is named exactly 1 times by the routes of every grid index. The 2 routes of a patch name different experts.
All inputs are finite; a program needn't handle non-finite values.
Results may differ from the reference program's by a relative error of at most 0.0051.
Values may be sent and summed in bfloat16 or wider, within the bound.
No kernel may reach another device: no remote copies, remote signals or barrier semaphores. Data moves between devices by JAX's collectives and lax.ppermute only.
A program may use at most 256 MiB of HBM per device.

```python
import jax
import jax.numpy as jnp
from jax import lax

C = 256
CG = 32
SIDE = 16
TOPK = 2
EXP_DEV = 8
PCOL = 4
PIX = 256
GROUPS = 8
EXPERTS = 128
BATCH = 2
NPATCH = 64
ROUTES = 16
N_GRID = 16
N_BATCH = 2


def draw_cotangent(key, part):
    channel_pos = jnp.arange(C, dtype=jnp.float32) / (C - 1)
    full_shape = (BATCH, C, NPATCH * PIX)
    channel_scale = 0.6 * 3.0 ** channel_pos
    values_drawn = jax.random.truncated_normal(key, -4.0, 4.0, full_shape, jnp.float32)
    return (values_drawn * channel_scale[None, :, None]).astype(jnp.bfloat16)


def draw_routes(key, part):
    hot_owner = jax.random.randint(jax.random.fold_in(key, 11), (), 0, N_GRID)
    tile_keys = jax.random.split(jax.random.fold_in(key, 12), N_GRID)
    owners = jax.vmap(lambda tile_key: jax.random.permutation(tile_key, N_GRID))(tile_keys)
    leading = owners[:, :1]
    owners = jnp.where(owners == hot_owner, leading, owners)
    position = jnp.arange(N_GRID)[None, :]
    owners = jnp.where(position == 0, hot_owner, owners)
    order_keys = jax.random.split(jax.random.fold_in(key, 13), N_GRID)
    route_order = jax.vmap(lambda tile_key: jax.random.permutation(tile_key, ROUTES))(order_keys)
    owner_of = jnp.take_along_axis(owners, route_order % N_GRID, axis=1)
    local_base = jax.random.randint(jax.random.fold_in(key, 14), (N_GRID, BATCH * PCOL, 1), 0, EXP_DEV)
    stride = 2 * jax.random.randint(jax.random.fold_in(key, 15), (N_GRID, BATCH * PCOL, 1), 0, max(EXP_DEV // 2, 1)) + 1
    local_index = (local_base + stride * jnp.arange(TOPK)[None, None, :]) % EXP_DEV
    experts = owner_of.reshape(N_GRID, BATCH * PCOL, TOPK) * EXP_DEV + local_index
    experts = experts.reshape(N_GRID, BATCH, PCOL, TOPK).transpose(1, 0, 2, 3)
    return experts.reshape(BATCH, NPATCH, TOPK).astype(jnp.int32)


def levels(stream_key, extent, cuts, least, top_value):
    loudness = 1.0
    for dim, blocks in cuts:
        draws = jax.random.uniform(jax.random.fold_in(jax.random.fold_in(stream_key, 6), dim), (blocks,), jnp.float32, least / len(cuts), top_value / len(cuts))
        loudness = loudness * jnp.repeat(jnp.exp(draws), extent[dim] // blocks).reshape((-1,) + (1,) * (len(extent) - 1 - dim))
    return loudness


def bell_draw(stream_key, shape, scale, reach, cuts=(), held_as=jnp.bfloat16):
    loudness = levels(stream_key, shape, cuts, -0.22, 0.18) if cuts else 1.0
    entries = jax.random.normal(stream_key, shape, jnp.float32) * scale * loudness
    return jnp.minimum(jnp.maximum(entries, -reach), reach).astype(held_as)


def setup_inputs(seed: int = 0) -> dict:
    key_of = jax.random.split(jax.random.key(seed), 6)
    inputs = bell_draw(key_of[0], (BATCH, C, NPATCH * PIX), 1.0, 6.0, ((0, 2), (2, 16)))
    cotangent = draw_cotangent(jax.random.fold_in(key_of[5], 71), 0)
    weights = bell_draw(key_of[2], (EXPERTS, GROUPS, CG * CG * 9), (9 * CG) ** -0.5, 0.375, ((0, 16), (1, 2)))
    gate_logits = bell_draw(key_of[3], (BATCH, NPATCH, TOPK), 1.5, 5.0, (), jnp.float32)
    routes = draw_routes(jax.random.fold_in(key_of[5], 71), 0)
    return {"inputs": inputs, "cotangent": cotangent, "weights": weights, "gate_logits": gate_logits, "routes": routes}


def shifted(values, row_shift, column_shift):
    margin = SIDE + 1
    padded = jnp.pad(values, [(0, 0)] * (values.ndim - 1) + [(margin, margin)])
    first_index = margin + row_shift * SIDE + column_shift
    moved = lax.slice_in_dim(padded, first_index, first_index + PIX, axis=values.ndim - 1)
    column = jnp.arange(PIX) % SIDE
    inside = ((column + column_shift >= 0) & (column + column_shift < SIDE)).astype(values.dtype)
    return moved * inside


def reference(inputs, cotangent, weights, gate_logits, routes):
    highest = lax.Precision.HIGHEST
    gate_values = jax.nn.sigmoid(gate_logits)
    w_table = weights.astype(jnp.float32).reshape(EXPERTS, GROUPS, CG, CG, 9)

    def per_sample(grad_total, sample_data):
        x_sample, dy_sample, route_ids, sample_gates = sample_data
        x_patches = x_sample.astype(jnp.float32).reshape(GROUPS, CG, NPATCH, PIX).transpose(2, 0, 1, 3)
        dy_patches = dy_sample.astype(jnp.float32).reshape(GROUPS, CG, NPATCH, PIX).transpose(2, 0, 1, 3)
        dx_total = jnp.zeros(x_patches.shape, jnp.float32)
        dot_list = []
        for rank_index in range(TOPK):
            kernels = w_table[route_ids[:, rank_index]]
            expert_image = jnp.zeros(x_patches.shape, jnp.float32)
            adjoint = jnp.zeros(x_patches.shape, jnp.float32)
            tap_grads = []
            for offset in range(9):
                row_shift = offset // 3 - 1
                column_shift = offset % 3 - 1
                tap_kernel = kernels[..., offset]
                moved_x = shifted(x_patches, row_shift, column_shift)
                expert_image = expert_image + jnp.einsum("ngoi,ngip->ngop", tap_kernel, moved_x, precision=highest)
                adjoint = adjoint + jnp.einsum("ngoi,ngop->ngip", tap_kernel, shifted(dy_patches, -row_shift, -column_shift), precision=highest)
                tap_grads.append(jnp.einsum("ngop,ngip->ngoi", dy_patches, moved_x, precision=highest))
            block_dots = jnp.sum((dy_patches * expert_image).reshape(NPATCH, N_BATCH, -1), axis=2)
            block_dots = lax.optimization_barrier(block_dots.astype(jnp.bfloat16)).astype(jnp.float32)
            dot_list.append(jnp.sum(block_dots, axis=1))
            route_gate = sample_gates[:, rank_index]
            gated_term = (route_gate[:, None, None, None] * adjoint).astype(jnp.bfloat16)
            dx_total = dx_total + lax.optimization_barrier(gated_term).astype(jnp.float32)
            route_grad = jnp.stack(tap_grads, axis=-1) * route_gate[:, None, None, None, None]
            grad_total = grad_total.at[route_ids[:, rank_index]].add(route_grad)
        dx_sample = dx_total.transpose(1, 2, 0, 3).reshape(C, NPATCH * PIX).astype(jnp.bfloat16)
        route_dots = jnp.stack(dot_list, axis=1)
        gate_grad = sample_gates * (1.0 - sample_gates) * route_dots / SIDE
        return grad_total, (dx_sample, gate_grad)

    zero_grads = jnp.zeros((EXPERTS, GROUPS, CG, CG, 9), jnp.float32)
    grad_total, (d_inputs, gate_grad) = lax.scan(per_sample, zero_grads, (inputs, cotangent, routes, gate_values))
    d_weights = (grad_total / SIDE).reshape(EXPERTS, GROUPS, CG * CG * 9)
    return d_inputs, d_weights, gate_grad
```

```python
import functools

import jax
import jax.numpy as jnp
from jax import lax
from jax.experimental import pallas as pl
from jax.experimental.pallas import tpu as pltpu
from jax.sharding import PartitionSpec as P

CG = 32
SIDE = 16
PIX = SIDE * SIDE
TAPS = 9
ROW = CG * TAPS
WIDE = 384
QUAD = 4 * ROW
ROWS = 8
DOT_ROWS = 16
VMEM_LIMIT = 48 * 1024 * 1024


def rolled(values, shift):
    extent = values.shape[1]
    shift %= extent
    return values if shift == 0 else pltpu.roll(values, shift, 1)


def pixel_masks(rows):
    pixel = lax.broadcasted_iota(jnp.int32, (rows, PIX), 1)
    column = pixel % SIDE
    return {
        "row": {-1: pixel >= SIDE, 1: pixel < PIX - SIDE},
        "column": {-1: column > 0, 1: column < SIDE - 1},
    }


def moved(values, row_shift, column_shift, masks):
    out = rolled(values, -(row_shift * SIDE + column_shift))
    if row_shift:
        out = jnp.where(masks["row"][row_shift], out, 0.0)
    if column_shift:
        out = jnp.where(masks["column"][column_shift], out, 0.0)
    return out


def joined(ref, start, count):
    return jnp.concatenate([ref[m, start:start + count, :] for m in range(ref.shape[0])], axis=1)


def strided(ref, start, count, stride):
    return jnp.concatenate(
        [ref[m, pl.ds(start, count, stride=stride), :] for m in range(ref.shape[0])], axis=1
    )


def put(ref, start, values):
    for at in range(0, values.shape[1], 128):
        piece = values[:, at:at + 128]
        ref[at // 128, start:start + values.shape[0], :piece.shape[1]] = piece


def pick_kernel(
    routes_ref, logits_ref, weights_ref, x_ref, dy_ref, wire_ref, send_ref, local_ref, logit_ref,
    wire_sem, send_sem,
):
    samples, top_count, patches = routes_ref.shape
    owned = weights_ref.shape[0]
    tiles = wire_ref.shape[0]
    others, _, channels, _ = send_ref.shape
    per_tile = patches // tiles
    first = lax.axis_index("grid") * owned
    mine = lax.axis_index("batch")

    def wire_copy(tile, local):
        return pltpu.make_async_copy(weights_ref.at[local], wire_ref.at[tile], wire_sem.at[tile])

    def send_copies(step):
        block = lax.rem(mine + step, others + 1)
        rows = pl.ds(pl.multiple_of(block * channels, channels), channels)
        return [
            pltpu.make_async_copy(
                source.at[0, rows], send_ref.at[step - 1, which], send_sem.at[step - 1, which]
            )
            for which, source in enumerate((x_ref, dy_ref))
        ]

    def pick(tile, carry):
        local = jnp.int32(0)
        logit = jnp.float32(0)
        for sample in range(samples):
            for place in range(per_tile):
                for rank in range(top_count):
                    patch = tile * per_tile + place
                    inside = routes_ref[sample, rank, patch] - first
                    hit = (inside >= 0) & (inside < owned)
                    local = jnp.where(hit, inside, local)
                    logit = jnp.where(hit, logits_ref[sample, rank, patch], logit)
        wire_copy(tile, local).start()
        local_ref[tile] = local
        logit_ref[tile] = logit
        return carry

    lax.fori_loop(0, tiles, pick, 0)
    for step in range(1, others + 1):
        for copy in send_copies(step):
            copy.start()

    def finish(tile, carry):
        wire_copy(tile, 0).wait()
        return carry

    lax.fori_loop(0, tiles, finish, 0)
    for step in range(1, others + 1):
        for copy in send_copies(step):
            copy.wait()


def grads_kernel(
    owned, routes_ref, x_ref, dy_ref, got_ref, wire_ref, dy_all_ref, x_all_ref, taps_ref, grad_ref
):
    samples, top_count, patches = routes_ref.shape
    tiles, groups, _ = wire_ref.shape
    others, _, channels, _ = got_ref.shape
    per_tile = patches // tiles
    together = ROWS // groups
    tile = lax.axis_index("grid")
    mine = lax.axis_index("batch")
    own_rows = pl.ds(pl.multiple_of(mine * channels, channels), channels)
    for place in range(per_tile):
        span = slice(place * PIX, (place + 1) * PIX)
        x_all_ref[mine * per_tile + place] = x_ref[0, own_rows, span]
        dy_all_ref[mine * per_tile + place] = dy_ref[0, own_rows, span]
        for step in range(1, others + 1):
            sample = lax.rem(mine - step + others + 1, others + 1)
            x_all_ref[sample * per_tile + place] = got_ref[step - 1, 0, :, span]
            dy_all_ref[sample * per_tile + place] = got_ref[step - 1, 1, :, span]
    grad_ref[WIDE // 128 - 1] = jnp.zeros((ROWS * CG, 128), jnp.float32)
    masks = pixel_masks(CG)

    def work(block, carry):
        for unit in range(ROWS):
            patch = block * together + unit // groups
            rows = slice((unit % groups) * CG, (unit % groups + 1) * CG)
            x_unit = x_all_ref[patch, rows, :].astype(jnp.float32)
            for tap in range(TAPS):
                part = moved(x_unit, tap // 3 - 1, tap % 3 - 1, masks)
                for half in range(PIX // 128):
                    taps_ref[half, pl.ds(unit * ROW + tap, CG, stride=TAPS), :] = part[
                        :, half * 128:(half + 1) * 128
                    ]
            grad = lax.dot_general(
                dy_all_ref[patch, rows, :],
                joined(taps_ref, unit * ROW, ROW).astype(jnp.bfloat16),
                (((1,), (1,)), ((), ())),
                preferred_element_type=jnp.float32,
            )
            put(grad_ref, unit * CG, grad)
        slots = []
        for place in range(together):
            patch = block * together + place
            column = tile * per_tile + lax.rem(patch, per_tile)
            slots.append(
                [
                    lax.div(routes_ref[lax.div(patch, per_tile), rank, column], owned)
                    for rank in range(top_count)
                ]
            )
        for quad in range(CG // 4):
            parts = [None] * TAPS
            for j in range(4):
                line = rolled(strided(grad_ref, quad * 4 + j, ROWS, CG), 32 * j)
                for m in range(3):
                    piece = line[:, m * 128:(m + 1) * 128]
                    at = 2 * j + m
                    parts[at] = piece if parts[at] is None else parts[at] + piece
            flat = jnp.concatenate(parts, axis=1)
            for place in range(together):
                value = flat[place * groups:(place + 1) * groups].astype(jnp.bfloat16)
                for slot in slots[place]:
                    wire_ref[slot, :, quad * QUAD:(quad + 1) * QUAD] = value
        return carry

    lax.fori_loop(0, samples * per_tile // together, work, 0)


def adjoint_kernel(
    owned, routes_ref, logits_ref, kernels_ref, grads_ref, dy_all_ref, out_ref,
    flat_ref, mixed_ref, spread_ref, dots_ref,
):
    samples, top_count, patches = routes_ref.shape
    tiles, groups, _ = kernels_ref.shape
    channels = groups * CG
    per_tile = patches // tiles
    together = ROWS // groups
    blocks = samples * per_tile // together
    tile = lax.axis_index("grid")
    mine = lax.axis_index("batch")
    masks = pixel_masks(CG)

    def work(block, carry):
        for place in range(together):
            patch = block * together + place
            sample = lax.div(patch, per_tile)
            column = tile * per_tile + lax.rem(patch, per_tile)
            gates, slots = [], []
            for rank in range(top_count):
                logit = logits_ref[sample, rank, column]
                gates.append(jax.nn.sigmoid(jnp.full((groups, 128), logit, jnp.float32)))
                slots.append(lax.div(routes_ref[sample, rank, column], owned))
            dots = [jnp.zeros((groups, 128), jnp.float32) for _ in range(top_count)]
            for at in range(0, CG * ROW, 128):
                lanes = slice(at, at + 128)
                mixed = jnp.zeros((groups, 128), jnp.float32)
                for rank in range(top_count):
                    kernel = kernels_ref[slots[rank], :, lanes].astype(jnp.float32)
                    grad = grads_ref[slots[rank], :, lanes].astype(jnp.float32)
                    dots[rank] += kernel * grad
                    mixed += gates[rank] * kernel
                flat_ref[place * groups:(place + 1) * groups, lanes] = mixed
            for rank in range(top_count):
                start = (block * top_count + rank) * ROWS + place * groups
                dots_ref[pl.ds(start, groups), :] = dots[rank]
        for quad in range(CG // 4):
            for j in range(4):
                start = quad * QUAD + 2 * j * 128
                line = rolled(flat_ref[:, start:start + WIDE], -32 * j)
                for m in range(WIDE // 128):
                    mixed_ref[m, pl.ds(quad * 4 + j, ROWS, stride=CG), :] = line[
                        :, m * 128:(m + 1) * 128
                    ]
        for unit in range(ROWS):
            patch = block * together + unit // groups
            rows = slice((unit % groups) * CG, (unit % groups + 1) * CG)
            kernel = joined(mixed_ref, unit * CG, CG)[:, :ROW].astype(jnp.bfloat16)
            spread = lax.dot_general(
                kernel,
                dy_all_ref[patch, rows, :],
                (((0,), (0,)), ((), ())),
                preferred_element_type=jnp.float32,
            )
            put(spread_ref, unit * ROW, spread)
            total = jnp.zeros((CG, PIX), jnp.float32)
            for tap in range(TAPS):
                part = strided(spread_ref, unit * ROW + tap, CG, TAPS)
                total += moved(part, 1 - tap // 3, 1 - tap % 3, masks)
            step = lax.rem(lax.div(patch, per_tile) - mine + samples, samples)
            offset = pl.multiple_of(lax.rem(patch, per_tile) * PIX, PIX)
            out_ref[step, rows, pl.ds(offset, PIX)] = total.astype(jnp.bfloat16)
        return carry

    lax.fori_loop(0, blocks, work, 0)
    count = blocks * top_count * ROWS
    sums = lax.dot_general(
        jnp.ones((DOT_ROWS, 128), jnp.float32),
        dots_ref[...],
        (((1,), (1,)), ((), ())),
        precision=lax.Precision.HIGHEST,
        preferred_element_type=jnp.float32,
    )
    row = lax.broadcasted_iota(jnp.int32, (count, 128), 0)
    lane = lax.broadcasted_iota(jnp.int32, (count, 128), 1)
    row_patch = row // (top_count * ROWS) * together + row % ROWS // groups
    row_rank = row // ROWS % top_count
    chosen = (lane == row_patch * top_count + row_rank).astype(jnp.float32)
    route_dots = lax.dot_general(
        sums,
        chosen,
        (((1,), (0,)), ((), ())),
        precision=lax.Precision.HIGHEST,
        preferred_element_type=jnp.float32,
    ).astype(jnp.bfloat16)
    for step in range(samples):
        out_ref[step, channels:channels + DOT_ROWS, :128] = route_dots


def sum_kernel(local_ref, logit_ref, got_ref, out_ref):
    tiles, groups, width = got_ref.shape
    out_ref[...] = jnp.zeros(out_ref.shape, jnp.float32)

    def add(tile, carry):
        local = local_ref[tile]
        gate = jax.nn.sigmoid(jnp.full((groups, 128), logit_ref[tile], jnp.float32)) / SIDE
        for at in range(0, width, 128):
            lanes = slice(at, at + 128)
            out_ref[local, :, lanes] += gate * got_ref[tile, :, lanes].astype(jnp.float32)
        return carry

    lax.fori_loop(0, tiles, add, 0)


def per_device(inputs, cotangent, weights, gate_logits, routes):
    tiles = lax.axis_size("grid")
    batch = lax.axis_size("batch")
    owned, groups, width = weights.shape
    samples, patches, top_count = routes.shape
    per_tile = patches // tiles
    span = inputs.shape[2]
    channels = groups * CG
    assert samples * per_tile * top_count == tiles and samples == batch
    smem = pl.BlockSpec(memory_space=pltpu.SMEM)
    vmem = pl.BlockSpec(memory_space=pltpu.VMEM)
    hbm = pl.BlockSpec(memory_space=pl.ANY)
    params = pltpu.CompilerParams(vmem_limit_bytes=VMEM_LIMIT)
    routes_t = routes.transpose(0, 2, 1)
    logits_t = gate_logits.transpose(0, 2, 1)
    wire_shape = jax.ShapeDtypeStruct((tiles, groups, width), jnp.bfloat16)

    picked, to_send, local, logit = pl.pallas_call(
        pick_kernel,
        out_shape=(
            wire_shape,
            jax.ShapeDtypeStruct((batch - 1, 2, channels, span), jnp.bfloat16),
            jax.ShapeDtypeStruct((tiles,), jnp.int32),
            jax.ShapeDtypeStruct((tiles,), jnp.float32),
        ),
        in_specs=[smem, smem, hbm, hbm, hbm],
        out_specs=(hbm, hbm, smem, smem),
        scratch_shapes=[
            pltpu.SemaphoreType.DMA((tiles,)),
            pltpu.SemaphoreType.DMA((batch - 1, 2)),
        ],
        compiler_params=params,
        name="pick",
    )(routes_t, logits_t, weights, inputs, cotangent)

    def exchange(blocks):
        return [
            lax.ppermute(
                blocks[step - 1], "batch", [(i, (i + step) % batch) for i in range(batch)]
            )
            for step in range(1, batch)
        ]

    kernels = lax.all_to_all(picked, "grid", split_axis=0, concat_axis=0, tiled=True)
    got = jnp.stack(exchange([to_send[step] for step in range(batch - 1)]))

    work = samples * patches // tiles * groups * width * PIX * 2
    grads, dy_all = pl.pallas_call(
        functools.partial(grads_kernel, owned),
        out_shape=(
            wire_shape,
            jax.ShapeDtypeStruct((samples * per_tile, channels, PIX), jnp.bfloat16),
        ),
        in_specs=[smem, vmem, vmem, vmem],
        out_specs=(vmem, vmem),
        scratch_shapes=[
            pltpu.VMEM((samples * per_tile, channels, PIX), jnp.bfloat16),
            pltpu.VMEM((PIX // 128, ROWS * ROW, 128), jnp.float32),
            pltpu.VMEM((WIDE // 128, ROWS * CG, 128), jnp.float32),
        ],
        compiler_params=params,
        cost_estimate=pl.CostEstimate(
            flops=work * 10, bytes_accessed=4 * 1024 * 1024, transcendentals=0
        ),
        name="kernel_grads",
    )(routes_t, inputs, cotangent, got)

    grads_back = lax.all_to_all(grads, "grid", split_axis=0, concat_axis=0, tiled=True)

    parts = pl.pallas_call(
        functools.partial(adjoint_kernel, owned),
        out_shape=jax.ShapeDtypeStruct((batch, channels + DOT_ROWS, span), jnp.bfloat16),
        in_specs=[smem, smem, vmem, vmem, vmem],
        out_specs=vmem,
        scratch_shapes=[
            pltpu.VMEM((ROWS, width), jnp.float32),
            pltpu.VMEM((WIDE // 128, ROWS * CG, 128), jnp.float32),
            pltpu.VMEM((PIX // 128, ROWS * ROW, 128), jnp.float32),
            pltpu.VMEM((samples * per_tile * top_count * groups, 128), jnp.float32),
        ],
        compiler_params=params,
        cost_estimate=pl.CostEstimate(
            flops=work * 10, bytes_accessed=4 * 1024 * 1024, transcendentals=0
        ),
        name="adjoint",
    )(routes_t, logits_t, kernels, grads, dy_all)

    arrived = exchange([parts[step] for step in range(1, batch)])
    mine = lax.axis_index("batch")
    d_inputs = jnp.zeros(inputs.shape, jnp.bfloat16)
    dots = jnp.zeros((128,), jnp.float32)
    for step, part in enumerate([parts[0]] + arrived):
        block = lax.rem(mine - step + batch, batch)
        d_inputs = lax.dynamic_update_slice(
            d_inputs, part[None, :channels], (0, block * channels, 0)
        )
        dots += part[channels, :128].astype(jnp.float32)
    dots = dots[:tiles].reshape(samples, per_tile, top_count)
    gates = jax.nn.sigmoid(
        lax.dynamic_slice_in_dim(gate_logits, lax.axis_index("grid") * per_tile, per_tile, 1)
    )
    gate_grad = gates * (1.0 - gates) * dots / SIDE

    d_weights = pl.pallas_call(
        sum_kernel,
        out_shape=jax.ShapeDtypeStruct(weights.shape, jnp.float32),
        in_specs=[smem, smem, vmem],
        out_specs=vmem,
        compiler_params=params,
        name="weight_sum",
    )(local, logit, grads_back)
    return (d_inputs, d_weights, gate_grad)


def solution(mesh):
    placed = (
        P("batch", None, "grid"),
        P("batch", None, "grid"),
        P("grid", "batch", None),
        P(),
        P(),
    )
    return jax.shard_map(
        per_device,
        mesh=mesh,
        in_specs=placed,
        out_specs=(P("batch", None, "grid"), P("grid", "batch", None), P(None, "grid", None)),
        check_vma=False,
    )
```

```python
import functools

import jax
import jax.numpy as jnp
from jax import lax
from jax.experimental import pallas as pl
from jax.experimental.pallas import tpu as pltpu
from jax.sharding import PartitionSpec as P

CG = 32
SIDE = 16
PIX = SIDE * SIDE
TAPS = 9
ROW = CG * TAPS
WIDE = 384
QUAD = 4 * ROW
ROWS = 8
DOT_ROWS = 16
VMEM_LIMIT = 48 * 1024 * 1024
WHOLE_VMEM = 60 * 1024 * 1024


def rolled(values, shift):
    extent = values.shape[1]
    shift %= extent
    return values if shift == 0 else pltpu.roll(values, shift, 1)


def pixel_masks(rows):
    pixel = lax.broadcasted_iota(jnp.int32, (rows, PIX), 1)
    column = pixel % SIDE
    return {
        "row": {-1: pixel >= SIDE, 1: pixel < PIX - SIDE},
        "column": {-1: column > 0, 1: column < SIDE - 1},
    }


def moved(values, row_shift, column_shift, masks):
    out = rolled(values, -(row_shift * SIDE + column_shift))
    if row_shift:
        out = jnp.where(masks["row"][row_shift], out, 0.0)
    if column_shift:
        out = jnp.where(masks["column"][column_shift], out, 0.0)
    return out


def joined(ref, start, count):
    return jnp.concatenate([ref[m, start:start + count, :] for m in range(ref.shape[0])], axis=1)


def strided(ref, start, count, stride):
    return jnp.concatenate(
        [ref[m, pl.ds(start, count, stride=stride), :] for m in range(ref.shape[0])], axis=1
    )


def put(ref, start, values):
    for at in range(0, values.shape[1], 128):
        piece = values[:, at:at + 128]
        ref[at // 128, start:start + values.shape[0], :piece.shape[1]] = piece


def pick_kernel(
    routes_hbm, logits_hbm, weights_hbm, x_hbm, dy_hbm, wire_ref, send_ref, local_ref, logit_ref,
    routes_ref, logits_ref, weights_ref, halves_ref, table_sem, weights_sem, halves_sem, wire_sem,
    send_sem,
):
    samples, top_count, patches = routes_ref.shape
    owned = weights_ref.shape[0]
    tiles = wire_ref.shape[0]
    others, _, channels, _ = send_ref.shape
    per_tile = patches // tiles
    first = lax.axis_index("grid") * owned
    mine = lax.axis_index("batch")
    tables = [
        pltpu.make_async_copy(routes_hbm, routes_ref, table_sem.at[0]),
        pltpu.make_async_copy(logits_hbm, logits_ref, table_sem.at[1]),
    ]
    fetched = pltpu.make_async_copy(weights_hbm, weights_ref, weights_sem)
    taken, sent = [], []
    for step in range(1, others + 1):
        block = lax.rem(mine + step, others + 1)
        rows = pl.ds(pl.multiple_of(block * channels, channels), channels)
        for which, source in enumerate((x_hbm, dy_hbm)):
            at = (step - 1, which)
            taken.append(
                pltpu.make_async_copy(source.at[0, rows], halves_ref.at[at], halves_sem.at[at])
            )
            sent.append(
                pltpu.make_async_copy(halves_ref.at[at], send_ref.at[at], send_sem.at[at])
            )
    for copy in tables + [fetched] + taken:
        copy.start()
    for copy in tables:
        copy.wait()

    def wire_copy(tile, local):
        return pltpu.make_async_copy(weights_ref.at[local], wire_ref.at[tile], wire_sem.at[tile])

    def pick(tile, carry):
        local = jnp.int32(0)
        logit = jnp.float32(0)
        for sample in range(samples):
            for place in range(per_tile):
                for rank in range(top_count):
                    patch = tile * per_tile + place
                    inside = routes_ref[sample, rank, patch] - first
                    hit = (inside >= 0) & (inside < owned)
                    local = jnp.where(hit, inside, local)
                    logit = jnp.where(hit, logits_ref[sample, rank, patch], logit)
        local_ref[tile] = local
        logit_ref[tile] = logit
        return carry

    def send(tile, carry):
        wire_copy(tile, local_ref[tile]).start()
        return carry

    def finish(tile, carry):
        wire_copy(tile, 0).wait()
        return carry

    lax.fori_loop(0, tiles, pick, 0)
    fetched.wait()
    lax.fori_loop(0, tiles, send, 0)
    for copy in taken:
        copy.wait()
    for copy in sent:
        copy.start()
    lax.fori_loop(0, tiles, finish, 0)
    for copy in sent:
        copy.wait()


def grads_kernel(
    owned, routes_ref, x_ref, dy_ref, got_ref, wire_ref, dy_all_ref, x_all_ref, taps_ref, grad_ref
):
    samples, top_count, patches = routes_ref.shape
    tiles, groups, _ = wire_ref.shape
    others, _, channels, _ = got_ref.shape
    per_tile = patches // tiles
    together = ROWS // groups
    tile = lax.axis_index("grid")
    mine = lax.axis_index("batch")
    own_rows = pl.ds(pl.multiple_of(mine * channels, channels), channels)
    for place in range(per_tile):
        span = slice(place * PIX, (place + 1) * PIX)
        x_all_ref[mine * per_tile + place] = x_ref[0, own_rows, span]
        dy_all_ref[mine * per_tile + place] = dy_ref[0, own_rows, span]
        for step in range(1, others + 1):
            sample = lax.rem(mine - step + others + 1, others + 1)
            x_all_ref[sample * per_tile + place] = got_ref[step - 1, 0, :, span]
            dy_all_ref[sample * per_tile + place] = got_ref[step - 1, 1, :, span]
    grad_ref[WIDE // 128 - 1] = jnp.zeros((ROWS * CG, 128), jnp.float32)
    masks = pixel_masks(CG)

    def work(block, carry):
        for unit in range(ROWS):
            patch = block * together + unit // groups
            rows = slice((unit % groups) * CG, (unit % groups + 1) * CG)
            x_unit = x_all_ref[patch, rows, :].astype(jnp.float32)
            for tap in range(TAPS):
                part = moved(x_unit, tap // 3 - 1, tap % 3 - 1, masks)
                for half in range(PIX // 128):
                    taps_ref[half, pl.ds(unit * ROW + tap, CG, stride=TAPS), :] = part[
                        :, half * 128:(half + 1) * 128
                    ]
            grad = lax.dot_general(
                dy_all_ref[patch, rows, :],
                joined(taps_ref, unit * ROW, ROW).astype(jnp.bfloat16),
                (((1,), (1,)), ((), ())),
                preferred_element_type=jnp.float32,
            )
            put(grad_ref, unit * CG, grad)
        slots = []
        for place in range(together):
            patch = block * together + place
            column = tile * per_tile + lax.rem(patch, per_tile)
            slots.append(
                [
                    lax.div(routes_ref[lax.div(patch, per_tile), rank, column], owned)
                    for rank in range(top_count)
                ]
            )
        for quad in range(CG // 4):
            parts = [None] * TAPS
            for j in range(4):
                line = rolled(strided(grad_ref, quad * 4 + j, ROWS, CG), 32 * j)
                for m in range(3):
                    piece = line[:, m * 128:(m + 1) * 128]
                    at = 2 * j + m
                    parts[at] = piece if parts[at] is None else parts[at] + piece
            flat = jnp.concatenate(parts, axis=1)
            for place in range(together):
                value = flat[place * groups:(place + 1) * groups].astype(jnp.bfloat16)
                for slot in slots[place]:
                    wire_ref[slot, :, quad * QUAD:(quad + 1) * QUAD] = value
        return carry

    lax.fori_loop(0, samples * per_tile // together, work, 0)


def adjoint_kernel(
    owned, routes_ref, logits_ref, kernels_ref, grads_ref, dy_all_ref, out_ref,
    flat_ref, mixed_ref, spread_ref, dots_ref,
):
    samples, top_count, patches = routes_ref.shape
    tiles, groups, _ = kernels_ref.shape
    channels = groups * CG
    per_tile = patches // tiles
    together = ROWS // groups
    blocks = samples * per_tile // together
    tile = lax.axis_index("grid")
    mine = lax.axis_index("batch")
    masks = pixel_masks(CG)

    def work(block, carry):
        for place in range(together):
            patch = block * together + place
            sample = lax.div(patch, per_tile)
            column = tile * per_tile + lax.rem(patch, per_tile)
            gates, slots = [], []
            for rank in range(top_count):
                logit = logits_ref[sample, rank, column]
                gates.append(jax.nn.sigmoid(jnp.full((groups, 128), logit, jnp.float32)))
                slots.append(lax.div(routes_ref[sample, rank, column], owned))
            dots = [jnp.zeros((groups, 128), jnp.float32) for _ in range(top_count)]
            for at in range(0, CG * ROW, 128):
                lanes = slice(at, at + 128)
                mixed = jnp.zeros((groups, 128), jnp.float32)
                for rank in range(top_count):
                    kernel = kernels_ref[slots[rank], :, lanes].astype(jnp.float32)
                    grad = grads_ref[slots[rank], :, lanes].astype(jnp.float32)
                    dots[rank] += kernel * grad
                    mixed += gates[rank] * kernel
                flat_ref[place * groups:(place + 1) * groups, lanes] = mixed
            for rank in range(top_count):
                start = (block * top_count + rank) * ROWS + place * groups
                dots_ref[pl.ds(start, groups), :] = dots[rank]
        for quad in range(CG // 4):
            for j in range(4):
                start = quad * QUAD + 2 * j * 128
                line = rolled(flat_ref[:, start:start + WIDE], -32 * j)
                for m in range(WIDE // 128):
                    mixed_ref[m, pl.ds(quad * 4 + j, ROWS, stride=CG), :] = line[
                        :, m * 128:(m + 1) * 128
                    ]
        for unit in range(ROWS):
            patch = block * together + unit // groups
            rows = slice((unit % groups) * CG, (unit % groups + 1) * CG)
            kernel = joined(mixed_ref, unit * CG, CG)[:, :ROW].astype(jnp.bfloat16)
            spread = lax.dot_general(
                kernel,
                dy_all_ref[patch, rows, :],
                (((0,), (0,)), ((), ())),
                preferred_element_type=jnp.float32,
            )
            put(spread_ref, unit * ROW, spread)
            total = jnp.zeros((CG, PIX), jnp.float32)
            for tap in range(TAPS):
                part = strided(spread_ref, unit * ROW + tap, CG, TAPS)
                total += moved(part, 1 - tap // 3, 1 - tap % 3, masks)
            step = lax.rem(lax.div(patch, per_tile) - mine + samples, samples)
            offset = pl.multiple_of(lax.rem(patch, per_tile) * PIX, PIX)
            out_ref[step, rows, pl.ds(offset, PIX)] = total.astype(jnp.bfloat16)
        return carry

    lax.fori_loop(0, blocks, work, 0)
    count = blocks * top_count * ROWS
    sums = lax.dot_general(
        jnp.ones((DOT_ROWS, 128), jnp.float32),
        dots_ref[...],
        (((1,), (1,)), ((), ())),
        precision=lax.Precision.HIGHEST,
        preferred_element_type=jnp.float32,
    )
    row = lax.broadcasted_iota(jnp.int32, (count, 128), 0)
    lane = lax.broadcasted_iota(jnp.int32, (count, 128), 1)
    row_patch = row // (top_count * ROWS) * together + row % ROWS // groups
    row_rank = row // ROWS % top_count
    chosen = (lane == row_patch * top_count + row_rank).astype(jnp.float32)
    route_dots = lax.dot_general(
        sums,
        chosen,
        (((1,), (0,)), ((), ())),
        precision=lax.Precision.HIGHEST,
        preferred_element_type=jnp.float32,
    ).astype(jnp.bfloat16)
    for step in range(samples):
        out_ref[step, channels:channels + DOT_ROWS, :128] = route_dots


def sum_kernel(local_ref, logit_ref, got_ref, out_ref):
    tiles, groups, width = got_ref.shape
    out_ref[...] = jnp.zeros(out_ref.shape, jnp.float32)

    def add(tile, carry):
        local = local_ref[tile]
        gate = jax.nn.sigmoid(jnp.full((groups, 128), logit_ref[tile], jnp.float32)) / SIDE
        for at in range(0, width, 128):
            lanes = slice(at, at + 128)
            out_ref[local, :, lanes] += gate * got_ref[tile, :, lanes].astype(jnp.float32)
        return carry

    lax.fori_loop(0, tiles, add, 0)


def per_device(inputs, cotangent, weights, gate_logits, routes):
    tiles = lax.axis_size("grid")
    batch = lax.axis_size("batch")
    owned, groups, width = weights.shape
    samples, patches, top_count = routes.shape
    per_tile = patches // tiles
    span = inputs.shape[2]
    channels = groups * CG
    assert samples * per_tile * top_count == tiles and samples == batch
    smem = pl.BlockSpec(memory_space=pltpu.SMEM)
    vmem = pl.BlockSpec(memory_space=pltpu.VMEM)
    hbm = pl.BlockSpec(memory_space=pltpu.HBM)
    params = pltpu.CompilerParams(vmem_limit_bytes=VMEM_LIMIT)
    routes_t = routes.transpose(0, 2, 1)
    logits_t = gate_logits.transpose(0, 2, 1)
    wire_shape = jax.ShapeDtypeStruct((tiles, groups, width), jnp.bfloat16)

    picked, to_send, local, logit = pl.pallas_call(
        pick_kernel,
        out_shape=(
            wire_shape,
            jax.ShapeDtypeStruct((batch - 1, 2, channels, span), jnp.bfloat16),
            jax.ShapeDtypeStruct((tiles,), jnp.int32),
            jax.ShapeDtypeStruct((tiles,), jnp.float32),
        ),
        in_specs=[hbm] * 5,
        out_specs=(hbm, hbm, smem, smem),
        scratch_shapes=[
            pltpu.SMEM(routes_t.shape, jnp.int32),
            pltpu.SMEM(routes_t.shape, jnp.float32),
            pltpu.VMEM(weights.shape, jnp.bfloat16),
            pltpu.VMEM((batch - 1, 2, channels, span), jnp.bfloat16),
            pltpu.SemaphoreType.DMA((2,)),
            pltpu.SemaphoreType.DMA,
            pltpu.SemaphoreType.DMA((batch - 1, 2)),
            pltpu.SemaphoreType.DMA((tiles,)),
            pltpu.SemaphoreType.DMA((batch - 1, 2)),
        ],
        compiler_params=pltpu.CompilerParams(vmem_limit_bytes=WHOLE_VMEM),
        name="pick",
    )(routes_t, logits_t, weights, inputs, cotangent)

    def exchange(blocks):
        return [
            lax.ppermute(
                blocks[step - 1], "batch", [(i, (i + step) % batch) for i in range(batch)]
            )
            for step in range(1, batch)
        ]

    kernels = lax.all_to_all(picked, "grid", split_axis=0, concat_axis=0, tiled=True)
    got = jnp.stack(exchange([to_send[step] for step in range(batch - 1)]))

    work = samples * patches // tiles * groups * width * PIX * 2
    grads, dy_all = pl.pallas_call(
        functools.partial(grads_kernel, owned),
        out_shape=(
            wire_shape,
            jax.ShapeDtypeStruct((samples * per_tile, channels, PIX), jnp.bfloat16),
        ),
        in_specs=[smem, vmem, vmem, vmem],
        out_specs=(vmem, vmem),
        scratch_shapes=[
            pltpu.VMEM((samples * per_tile, channels, PIX), jnp.bfloat16),
            pltpu.VMEM((PIX // 128, ROWS * ROW, 128), jnp.float32),
            pltpu.VMEM((WIDE // 128, ROWS * CG, 128), jnp.float32),
        ],
        compiler_params=params,
        cost_estimate=pl.CostEstimate(
            flops=work * 10, bytes_accessed=4 * 1024 * 1024, transcendentals=0
        ),
        name="kernel_grads",
    )(routes_t, inputs, cotangent, got)

    grads_back = lax.all_to_all(grads, "grid", split_axis=0, concat_axis=0, tiled=True)

    parts = pl.pallas_call(
        functools.partial(adjoint_kernel, owned),
        out_shape=jax.ShapeDtypeStruct((batch, channels + DOT_ROWS, span), jnp.bfloat16),
        in_specs=[smem, smem, vmem, vmem, vmem],
        out_specs=vmem,
        scratch_shapes=[
            pltpu.VMEM((ROWS, width), jnp.float32),
            pltpu.VMEM((WIDE // 128, ROWS * CG, 128), jnp.float32),
            pltpu.VMEM((PIX // 128, ROWS * ROW, 128), jnp.float32),
            pltpu.VMEM((samples * per_tile * top_count * groups, 128), jnp.float32),
        ],
        compiler_params=params,
        cost_estimate=pl.CostEstimate(
            flops=work * 10, bytes_accessed=4 * 1024 * 1024, transcendentals=0
        ),
        name="adjoint",
    )(routes_t, logits_t, kernels, grads, dy_all)

    arrived = exchange([parts[step] for step in range(1, batch)])
    mine = lax.axis_index("batch")
    d_inputs = jnp.zeros(inputs.shape, jnp.bfloat16)
    dots = jnp.zeros((128,), jnp.float32)
    for step, part in enumerate([parts[0]] + arrived):
        block = lax.rem(mine - step + batch, batch)
        d_inputs = lax.dynamic_update_slice(
            d_inputs, part[None, :channels], (0, block * channels, 0)
        )
        dots += part[channels, :128].astype(jnp.float32)
    dots = dots[:tiles].reshape(samples, per_tile, top_count)
    gates = jax.nn.sigmoid(
        lax.dynamic_slice_in_dim(gate_logits, lax.axis_index("grid") * per_tile, per_tile, 1)
    )
    gate_grad = gates * (1.0 - gates) * dots / SIDE

    d_weights = pl.pallas_call(
        sum_kernel,
        out_shape=jax.ShapeDtypeStruct(weights.shape, jnp.float32),
        in_specs=[smem, smem, vmem],
        out_specs=vmem,
        compiler_params=params,
        name="weight_sum",
    )(local, logit, grads_back)
    return (d_inputs, d_weights, gate_grad)


def solution(mesh):
    placed = (
        P("batch", None, "grid"),
        P("batch", None, "grid"),
        P("grid", "batch", None),
        P(),
        P(),
    )
    return jax.shard_map(
        per_device,
        mesh=mesh,
        in_specs=placed,
        out_specs=(P("batch", None, "grid"), P("grid", "batch", None), P(None, "grid", None)),
        check_vma=False,
    )
```

```python
import functools

import jax
import jax.numpy as jnp
from jax import lax
from jax.experimental import pallas as pl
from jax.experimental.pallas import tpu as pltpu
from jax.sharding import PartitionSpec as P

CG = 32
SIDE = 16
PIX = SIDE * SIDE
TAPS = 9
ROW = CG * TAPS
WIDE = 384
QUAD = 4 * ROW
ROWS = 8
DOT_ROWS = 16
VMEM_LIMIT = 32 * 1024 * 1024
COST = 20_000_000_000
WHOLE_VMEM = 60 * 1024 * 1024


def rolled(values, shift):
    extent = values.shape[1]
    shift %= extent
    return values if shift == 0 else pltpu.roll(values, shift, 1)


def pixel_masks(rows):
    pixel = lax.broadcasted_iota(jnp.int32, (rows, PIX), 1)
    column = pixel % SIDE
    return {
        "row": {-1: pixel >= SIDE, 1: pixel < PIX - SIDE},
        "column": {-1: column > 0, 1: column < SIDE - 1},
    }


def moved(values, row_shift, column_shift, masks):
    out = rolled(values, -(row_shift * SIDE + column_shift))
    if row_shift:
        out = jnp.where(masks["row"][row_shift], out, 0.0)
    if column_shift:
        out = jnp.where(masks["column"][column_shift], out, 0.0)
    return out


def joined(ref, start, count):
    return jnp.concatenate([ref[m, start:start + count, :] for m in range(ref.shape[0])], axis=1)


def strided(ref, start, count, stride):
    return jnp.concatenate(
        [ref[m, pl.ds(start, count, stride=stride), :] for m in range(ref.shape[0])], axis=1
    )


def put(ref, start, values):
    for at in range(0, values.shape[1], 128):
        piece = values[:, at:at + 128]
        ref[at // 128, start:start + values.shape[0], :piece.shape[1]] = piece


def pair_order(tiles):
    near, far = list(range(tiles // 4)), list(range(tiles // 4, tiles // 2))
    return near[1:3] + far + near[3:] + near[:1]


def scan_kernel(
    owned, routes_hbm, logits_hbm, x_hbm, dy_hbm, send_ref, local_ref, logit_ref, beside_ref,
    routes_ref, logits_ref, halves_ref, table_sem, halves_sem, send_sem,
):
    samples, top_count, patches = routes_ref.shape
    tiles = local_ref.shape[0]
    others, _, channels, _ = send_ref.shape
    per_tile = patches // tiles
    here = lax.axis_index("grid")
    mine = lax.axis_index("batch")
    tables = [
        pltpu.make_async_copy(routes_hbm, routes_ref, table_sem.at[0]),
        pltpu.make_async_copy(logits_hbm, logits_ref, table_sem.at[1]),
    ]
    taken, sent = [], []
    for step in range(1, others + 1):
        block = lax.rem(mine + step, others + 1)
        rows = pl.ds(pl.multiple_of(block * channels, channels), channels)
        for which, source in enumerate((x_hbm, dy_hbm)):
            at = (step - 1, which)
            taken.append(
                pltpu.make_async_copy(source.at[0, rows], halves_ref.at[at], halves_sem.at[at])
            )
            sent.append(
                pltpu.make_async_copy(halves_ref.at[at], send_ref.at[at], send_sem.at[at])
            )
    for copy in tables + taken:
        copy.start()
    for copy in tables:
        copy.wait()
    for copy in taken:
        copy.wait()
    for copy in sent:
        copy.start()
    first = here * owned
    first_beside = (here ^ 1) * owned

    def scan(tile, carry):
        local, beside = jnp.int32(0), jnp.int32(0)
        logit = jnp.float32(0)
        for sample in range(samples):
            for place in range(per_tile):
                for rank in range(top_count):
                    patch = tile * per_tile + place
                    expert = routes_ref[sample, rank, patch]
                    inside = expert - first
                    hit = (inside >= 0) & (inside < owned)
                    local = jnp.where(hit, inside, local)
                    logit = jnp.where(hit, logits_ref[sample, rank, patch], logit)
                    inside = expert - first_beside
                    hit = (inside >= 0) & (inside < owned)
                    beside = jnp.where(hit, inside, beside)
        local_ref[tile] = local
        logit_ref[tile] = logit
        beside_ref[tile] = beside
        return carry

    lax.fori_loop(0, tiles, scan, 0)
    for copy in sent:
        copy.wait()


def pack_kernel(local_ref, beside_ref, own_hbm, beside_hbm, *rest):
    pair_refs, (own_ref, next_ref, fetch_sem, pair_sem) = rest[:-4], rest[-4:]
    here = lax.axis_index("grid")
    fetches = [
        pltpu.make_async_copy(own_hbm, own_ref, fetch_sem.at[0]),
        pltpu.make_async_copy(beside_hbm, next_ref, fetch_sem.at[1]),
    ]
    for copy in fetches:
        copy.start()
    copies = []
    for which, (ids, source) in enumerate(((local_ref, own_ref), (beside_ref, next_ref))):
        fetches[which].wait()
        for pair, target in zip(pair_order(2 * len(pair_refs)), pair_refs):
            copies.append(
                pltpu.make_async_copy(
                    source.at[ids[here ^ (2 * pair)]], target.at[which], pair_sem.at[pair, which]
                )
            )
            copies[-1].start()
    for copy in copies:
        copy.wait()


def grads_kernel(
    owned, routes_ref, x_ref, dy_ref, got_ref, wire_ref, grads_ref, dy_all_ref, x_all_ref, taps_ref,
    grad_ref,
):
    samples, top_count, patches = routes_ref.shape
    tiles, groups, _ = wire_ref.shape
    others, _, channels, _ = got_ref.shape
    per_tile = patches // tiles
    together = min(ROWS // groups, per_tile)
    rows_count = together * groups
    tile = lax.axis_index("grid")
    mine = lax.axis_index("batch")
    own_rows = pl.ds(pl.multiple_of(mine * channels, channels), channels)
    for place in range(per_tile):
        span = slice(place * PIX, (place + 1) * PIX)
        x_all_ref[mine * per_tile + place] = x_ref[0, own_rows, span]
        dy_all_ref[mine * per_tile + place] = dy_ref[0, own_rows, span]
        for step in range(1, others + 1):
            sample = lax.rem(mine - step + others + 1, others + 1)
            x_all_ref[sample * per_tile + place] = got_ref[step - 1, 0, :, span]
            dy_all_ref[sample * per_tile + place] = got_ref[step - 1, 1, :, span]
    grad_ref[WIDE // 128 - 1] = jnp.zeros((rows_count * CG, 128), jnp.float32)
    masks = pixel_masks(CG)

    def work(block, carry):
        for unit in range(rows_count):
            patch = block * together + unit // groups
            rows = slice((unit % groups) * CG, (unit % groups + 1) * CG)
            x_unit = x_all_ref[patch, rows, :].astype(jnp.float32)
            for tap in range(TAPS):
                part = moved(x_unit, tap // 3 - 1, tap % 3 - 1, masks)
                for half in range(PIX // 128):
                    taps_ref[half, pl.ds(unit * ROW + tap, CG, stride=TAPS), :] = part[
                        :, half * 128:(half + 1) * 128
                    ]
            grad = lax.dot_general(
                dy_all_ref[patch, rows, :],
                joined(taps_ref, unit * ROW, ROW).astype(jnp.bfloat16),
                (((1,), (1,)), ((), ())),
                preferred_element_type=jnp.float32,
            )
            put(grad_ref, unit * CG, grad)
        slots = []
        for place in range(together):
            patch = block * together + place
            column = tile * per_tile + lax.rem(patch, per_tile)
            slots.append([])
            for rank in range(top_count):
                expert = routes_ref[lax.div(patch, per_tile), rank, column]
                slots[-1].append(lax.div(expert, owned))
        for quad in range(CG // 4):
            parts = [None] * TAPS
            for j in range(4):
                line = rolled(strided(grad_ref, quad * 4 + j, rows_count, CG), 32 * j)
                for m in range(3):
                    piece = line[:, m * 128:(m + 1) * 128]
                    at = 2 * j + m
                    parts[at] = piece if parts[at] is None else parts[at] + piece
            flat = jnp.concatenate(parts, axis=1)
            for place in range(together):
                value = flat[place * groups:(place + 1) * groups].astype(jnp.bfloat16)
                lanes = slice(quad * QUAD, (quad + 1) * QUAD)
                grads_ref[block * together + place, :, lanes] = value
                for slot in slots[place]:
                    wire_ref[slot, :, lanes] = value
        return carry

    lax.fori_loop(0, samples * per_tile // together, work, 0)


def adjoint_kernel(
    owned, routes_ref, logits_ref, grads_ref, dy_all_ref, *rest
):
    pair_refs, rest = rest[:-7], rest[-7:]
    out_ref, kernels_ref, flat_ref, mixed_ref, spread_ref, dots_ref, place_sem = rest
    samples, top_count, patches = routes_ref.shape
    tiles, groups, _ = kernels_ref.shape
    channels = groups * CG
    per_tile = patches // tiles
    together = min(ROWS // groups, per_tile)
    rows_count = together * groups
    blocks = samples * per_tile // together
    tile = lax.axis_index("grid")
    mine = lax.axis_index("batch")
    places = [
        (source.at[which], kernels_ref.at[tile ^ (2 * pair + which)])
        for pair, source in zip(pair_order(tiles), pair_refs)
        for which in range(2)
    ]
    copies = [
        pltpu.make_async_copy(source, target, place_sem.at[number])
        for number, (source, target) in enumerate(places)
    ]
    for copy in copies:
        copy.start()
    masks = pixel_masks(CG)
    for copy in copies:
        copy.wait()

    def work(block, carry):
        for place in range(together):
            patch = block * together + place
            sample = lax.div(patch, per_tile)
            column = tile * per_tile + lax.rem(patch, per_tile)
            gates, slots = [], []
            for rank in range(top_count):
                logit = logits_ref[sample, rank, column]
                gates.append(jax.nn.sigmoid(jnp.full((groups, 128), logit, jnp.float32)))
                slots.append(lax.div(routes_ref[sample, rank, column], owned))
            dots = [jnp.zeros((groups, 128), jnp.float32) for _ in range(top_count)]
            for at in range(0, CG * ROW, 128):
                lanes = slice(at, at + 128)
                mixed = jnp.zeros((groups, 128), jnp.float32)
                grad = grads_ref[patch, :, lanes].astype(jnp.float32)
                for rank in range(top_count):
                    kernel = kernels_ref[slots[rank], :, lanes].astype(jnp.float32)
                    dots[rank] += kernel * grad
                    mixed += gates[rank] * kernel
                flat_ref[place * groups:(place + 1) * groups, lanes] = mixed
            for rank in range(top_count):
                start = (block * top_count + rank) * rows_count + place * groups
                dots_ref[pl.ds(start, groups), :] = dots[rank]
        for quad in range(CG // 4):
            for j in range(4):
                start = quad * QUAD + 2 * j * 128
                line = rolled(flat_ref[:, start:start + WIDE], -32 * j)
                for m in range(WIDE // 128):
                    mixed_ref[m, pl.ds(quad * 4 + j, rows_count, stride=CG), :] = line[
                        :, m * 128:(m + 1) * 128
                    ]
        for unit in range(rows_count):
            patch = block * together + unit // groups
            rows = slice((unit % groups) * CG, (unit % groups + 1) * CG)
            kernel = joined(mixed_ref, unit * CG, CG)[:, :ROW].astype(jnp.bfloat16)
            spread = lax.dot_general(
                kernel,
                dy_all_ref[patch, rows, :],
                (((0,), (0,)), ((), ())),
                preferred_element_type=jnp.float32,
            )
            put(spread_ref, unit * ROW, spread)
            total = jnp.zeros((CG, PIX), jnp.float32)
            for tap in range(TAPS):
                part = strided(spread_ref, unit * ROW + tap, CG, TAPS)
                total += moved(part, 1 - tap // 3, 1 - tap % 3, masks)
            step = lax.rem(lax.div(patch, per_tile) - mine + samples, samples)
            offset = pl.multiple_of(lax.rem(patch, per_tile) * PIX, PIX)
            out_ref[step, rows, pl.ds(offset, PIX)] = total.astype(jnp.bfloat16)
        return carry

    lax.fori_loop(0, blocks, work, 0)
    count = blocks * top_count * rows_count
    sums = lax.dot_general(
        jnp.ones((DOT_ROWS, 128), jnp.float32),
        dots_ref[...],
        (((1,), (1,)), ((), ())),
        precision=lax.Precision.HIGHEST,
        preferred_element_type=jnp.float32,
    )
    row = lax.broadcasted_iota(jnp.int32, (count, 128), 0)
    lane = lax.broadcasted_iota(jnp.int32, (count, 128), 1)
    row_patch = row // (top_count * rows_count) * together + row % rows_count // groups
    row_rank = row // rows_count % top_count
    chosen = (lane == row_patch * top_count + row_rank).astype(jnp.float32)
    route_dots = lax.dot_general(
        sums,
        chosen,
        (((1,), (0,)), ((), ())),
        precision=lax.Precision.HIGHEST,
        preferred_element_type=jnp.float32,
    ).astype(jnp.bfloat16)
    for step in range(samples):
        out_ref[step, channels:channels + DOT_ROWS, :128] = route_dots


def sum_kernel(local_ref, logit_ref, got_ref, out_ref):
    tiles, groups, width = got_ref.shape
    out_ref[...] = jnp.zeros(out_ref.shape, jnp.float32)

    def add(tile, carry):
        local = local_ref[tile]
        gate = jax.nn.sigmoid(jnp.full((groups, 128), logit_ref[tile], jnp.float32)) / SIDE
        for at in range(0, width, 128):
            lanes = slice(at, at + 128)
            out_ref[local, :, lanes] += gate * got_ref[tile, :, lanes].astype(jnp.float32)
        return carry

    lax.fori_loop(0, tiles, add, 0)


def per_device(inputs, cotangent, weights, gate_logits, routes):
    tiles = lax.axis_size("grid")
    batch = lax.axis_size("batch")
    owned, groups, width = weights.shape
    samples, patches, top_count = routes.shape
    per_tile = patches // tiles
    span = inputs.shape[2]
    channels = groups * CG
    assert samples * per_tile * top_count == tiles and samples == batch
    smem = pl.BlockSpec(memory_space=pltpu.SMEM)
    vmem = pl.BlockSpec(memory_space=pltpu.VMEM)
    hbm = pl.BlockSpec(memory_space=pltpu.HBM)
    anywhere = pl.BlockSpec(memory_space=pl.ANY)
    params = pltpu.CompilerParams(vmem_limit_bytes=VMEM_LIMIT)
    routes_t = routes.transpose(0, 2, 1)
    logits_t = gate_logits.transpose(0, 2, 1)
    assert tiles & (tiles - 1) == 0 and tiles > 1
    together = min(ROWS // groups, per_tile)
    rows = together * groups

    def blocks_shape(count):
        return jax.ShapeDtypeStruct((count, groups, width), jnp.bfloat16)

    def swap(blocks, step):
        return lax.ppermute(blocks, "grid", [(i, i ^ step) for i in range(tiles)])

    weights_beside = swap(weights, 1)
    table = jax.ShapeDtypeStruct((tiles,), jnp.int32)
    to_send, local, logit, beside = pl.pallas_call(
        functools.partial(scan_kernel, owned),
        out_shape=(
            jax.ShapeDtypeStruct((batch - 1, 2, channels, span), jnp.bfloat16),
            table,
            jax.ShapeDtypeStruct((tiles,), jnp.float32),
            table,
        ),
        in_specs=[hbm] * 4,
        out_specs=(hbm, smem, smem, smem),
        scratch_shapes=[
            pltpu.SMEM(routes_t.shape, jnp.int32),
            pltpu.SMEM(routes_t.shape, jnp.float32),
            pltpu.VMEM((batch - 1, 2, channels, span), jnp.bfloat16),
            pltpu.SemaphoreType.DMA((2,)),
            pltpu.SemaphoreType.DMA((batch - 1, 2)),
            pltpu.SemaphoreType.DMA((batch - 1, 2)),
        ],
        compiler_params=pltpu.CompilerParams(vmem_limit_bytes=WHOLE_VMEM),
        cost_estimate=pl.CostEstimate(flops=COST, bytes_accessed=1, transcendentals=0),
        name="scan",
    )(routes_t, logits_t, inputs, cotangent)

    pairs = pl.pallas_call(
        pack_kernel,
        out_shape=(blocks_shape(2),) * (tiles // 2),
        in_specs=[smem, smem, hbm, hbm],
        out_specs=(hbm,) * (tiles // 2),
        scratch_shapes=[
            pltpu.VMEM(weights.shape, jnp.bfloat16),
            pltpu.VMEM(weights.shape, jnp.bfloat16),
            pltpu.SemaphoreType.DMA((2,)),
            pltpu.SemaphoreType.DMA((tiles // 2, 2)),
        ],
        compiler_params=pltpu.CompilerParams(vmem_limit_bytes=WHOLE_VMEM),
        name="pack",
    )(local, beside, weights, weights_beside)
    pairs = [
        blocks if pair == 0 else swap(blocks, 2 * pair)
        for pair, blocks in zip(pair_order(tiles), pairs)
    ]

    def exchange(blocks):
        return [
            lax.ppermute(
                blocks[step - 1], "batch", [(i, (i + step) % batch) for i in range(batch)]
            )
            for step in range(1, batch)
        ]

    got = jnp.stack(exchange([to_send[step] for step in range(batch - 1)]))

    work = samples * patches // tiles * groups * width * PIX * 2
    wire, grads, dy_all = pl.pallas_call(
        functools.partial(grads_kernel, owned),
        out_shape=(
            blocks_shape(tiles),
            blocks_shape(samples * per_tile),
            jax.ShapeDtypeStruct((samples * per_tile, channels, PIX), jnp.bfloat16),
        ),
        in_specs=[smem, vmem, vmem, vmem],
        out_specs=(vmem, vmem, vmem),
        scratch_shapes=[
            pltpu.VMEM((samples * per_tile, channels, PIX), jnp.bfloat16),
            pltpu.VMEM((PIX // 128, rows * ROW, 128), jnp.float32),
            pltpu.VMEM((WIDE // 128, rows * CG, 128), jnp.float32),
        ],
        compiler_params=params,
        cost_estimate=pl.CostEstimate(flops=COST, bytes_accessed=1, transcendentals=0),
        name="kernel_grads",
    )(routes_t, inputs, cotangent, got)

    grads_back = lax.all_to_all(wire, "grid", split_axis=0, concat_axis=0, tiled=True)

    parts = pl.pallas_call(
        functools.partial(adjoint_kernel, owned),
        out_shape=jax.ShapeDtypeStruct((batch, channels + DOT_ROWS, span), jnp.bfloat16),
        in_specs=[smem, smem, vmem, vmem] + [anywhere] * (tiles // 2),
        out_specs=vmem,
        scratch_shapes=[
            pltpu.VMEM((tiles, groups, width), jnp.bfloat16),
            pltpu.VMEM((rows, width), jnp.float32),
            pltpu.VMEM((WIDE // 128, rows * CG, 128), jnp.float32),
            pltpu.VMEM((PIX // 128, rows * ROW, 128), jnp.float32),
            pltpu.VMEM((samples * per_tile * top_count * groups, 128), jnp.float32),
            pltpu.SemaphoreType.DMA((tiles,)),
        ],
        compiler_params=params,
        cost_estimate=pl.CostEstimate(flops=COST, bytes_accessed=1, transcendentals=0),
        name="adjoint",
    )(routes_t, logits_t, grads, dy_all, *pairs)

    arrived = exchange([parts[step] for step in range(1, batch)])
    mine = lax.axis_index("batch")
    d_inputs = jnp.zeros(inputs.shape, jnp.bfloat16)
    dots = jnp.zeros((128,), jnp.float32)
    for step, part in enumerate([parts[0]] + arrived):
        block = lax.rem(mine - step + batch, batch)
        d_inputs = lax.dynamic_update_slice(
            d_inputs, part[None, :channels], (0, block * channels, 0)
        )
        dots += part[channels, :128].astype(jnp.float32)
    dots = dots[:tiles].reshape(samples, per_tile, top_count)
    gates = jax.nn.sigmoid(
        lax.dynamic_slice_in_dim(gate_logits, lax.axis_index("grid") * per_tile, per_tile, 1)
    )
    gate_grad = gates * (1.0 - gates) * dots / SIDE

    d_weights = pl.pallas_call(
        sum_kernel,
        out_shape=jax.ShapeDtypeStruct(weights.shape, jnp.float32),
        in_specs=[smem, smem, vmem],
        out_specs=vmem,
        compiler_params=params,
        name="weight_sum",
    )(local, logit, grads_back)
    return (d_inputs, d_weights, gate_grad)


def solution(mesh):
    placed = (
        P("batch", None, "grid"),
        P("batch", None, "grid"),
        P("grid", "batch", None),
        P(),
        P(),
    )
    return jax.shard_map(
        per_device,
        mesh=mesh,
        in_specs=placed,
        out_specs=(P("batch", None, "grid"), P("grid", "batch", None), P(None, "grid", None)),
        check_vma=False,
    )
```

```python
import functools

import jax
import jax.numpy as jnp
from jax import lax
from jax.experimental import pallas as pl
from jax.experimental.pallas import tpu as pltpu
from jax.sharding import PartitionSpec as P

CG = 32
SIDE = 16
PIX = SIDE * SIDE
TAPS = 9
ROW = CG * TAPS
WIDE = 384
QUAD = 4 * ROW
ROWS = 8
DOT_ROWS = 16
VMEM_LIMIT = 16 * 1024 * 1024
SUM_CHUNKS = 3
COST = 20_000_000_000


def rolled(values, shift):
    extent = values.shape[1]
    shift %= extent
    return values if shift == 0 else pltpu.roll(values, shift, 1)


def pixel_masks(rows):
    pixel = lax.broadcasted_iota(jnp.int32, (rows, PIX), 1)
    column = pixel % SIDE
    return {
        "row": {-1: pixel >= SIDE, 1: pixel < PIX - SIDE},
        "column": {-1: column > 0, 1: column < SIDE - 1},
    }


def moved(values, row_shift, column_shift, masks):
    out = rolled(values, -(row_shift * SIDE + column_shift))
    if row_shift:
        out = jnp.where(masks["row"][row_shift], out, 0.0)
    if column_shift:
        out = jnp.where(masks["column"][column_shift], out, 0.0)
    return out


def joined(ref, start, count):
    return jnp.concatenate([ref[m, start:start + count, :] for m in range(ref.shape[0])], axis=1)


def strided(ref, start, count, stride):
    return jnp.concatenate(
        [ref[m, pl.ds(start, count, stride=stride), :] for m in range(ref.shape[0])], axis=1
    )


def put(ref, start, values):
    for at in range(0, values.shape[1], 128):
        piece = values[:, at:at + 128]
        ref[at // 128, start:start + values.shape[0], :piece.shape[1]] = piece


def pair_order(tiles):
    near, far = list(range(tiles // 4)), list(range(tiles // 4, tiles // 2))
    return near[1:3] + far + near[3:] + near[:1]


def named(routes_ref, tile, per_tile, first, owned):
    samples, top_count, _ = routes_ref.shape
    for sample in range(samples):
        for place in range(per_tile):
            for rank in range(top_count):
                at = (sample, rank, tile * per_tile + place)
                inside = routes_ref[at] - first
                yield at, inside, (inside >= 0) & (inside < owned)


def scan_kernel(owned, per_tile, routes_ref, local_ref, beside_ref):
    here = lax.axis_index("grid")

    def scan(pair, carry):
        tile = here ^ (2 * pair)
        for owner, found_ref in ((here, local_ref), (here ^ 1, beside_ref)):
            found = jnp.int32(0)
            for _, inside, hit in named(routes_ref, tile, per_tile, owner * owned, owned):
                found += jnp.where(hit, inside, 0)
            found_ref[pair] = found
        return carry

    lax.fori_loop(0, local_ref.shape[0], scan, 0)


def pack_kernel(local_ref, beside_ref, own_ref, next_ref, x_ref, dy_ref, send_ref, *rest):
    pair_refs, (pair_sem, send_sem) = rest[:-2], rest[-2:]
    others, _, channels, _ = send_ref.shape
    mine = lax.axis_index("batch")
    copies = [
        pltpu.make_async_copy(
            source.at[ids[pair]], target.at[which], pair_sem.at[pair, which]
        )
        for pair, target in zip(pair_order(2 * len(pair_refs)), pair_refs)
        for which, (ids, source) in enumerate(((local_ref, own_ref), (beside_ref, next_ref)))
    ]
    for step in range(1, others + 1):
        block = lax.rem(mine + step, others + 1)
        rows = pl.ds(pl.multiple_of(block * channels, channels), channels)
        for which, source in enumerate((x_ref, dy_ref)):
            at = (step - 1, which)
            copies.append(
                pltpu.make_async_copy(source.at[0, rows], send_ref.at[at], send_sem.at[at])
            )
    for copy in copies:
        copy.start()
    for copy in copies:
        copy.wait()


def grads_kernel(
    owned, routes_ref, x_ref, dy_ref, got_ref, wire_ref, grads_ref, dy_all_ref, x_all_ref, taps_ref,
    grad_ref,
):
    samples, top_count, patches = routes_ref.shape
    tiles, groups, _ = wire_ref.shape
    others, _, channels, _ = got_ref.shape
    per_tile = patches // tiles
    together = min(ROWS // groups, per_tile)
    rows_count = together * groups
    tile = lax.axis_index("grid")
    mine = lax.axis_index("batch")
    own_rows = pl.ds(pl.multiple_of(mine * channels, channels), channels)
    for place in range(per_tile):
        span = slice(place * PIX, (place + 1) * PIX)
        x_all_ref[mine * per_tile + place] = x_ref[0, own_rows, span]
        dy_all_ref[mine * per_tile + place] = dy_ref[0, own_rows, span]
        for step in range(1, others + 1):
            sample = lax.rem(mine - step + others + 1, others + 1)
            x_all_ref[sample * per_tile + place] = got_ref[step - 1, 0, :, span]
            dy_all_ref[sample * per_tile + place] = got_ref[step - 1, 1, :, span]
    grad_ref[WIDE // 128 - 1] = jnp.zeros((rows_count * CG, 128), jnp.float32)
    masks = pixel_masks(CG)

    def work(block, carry):
        for unit in range(rows_count):
            patch = block * together + unit // groups
            rows = slice((unit % groups) * CG, (unit % groups + 1) * CG)
            x_unit = x_all_ref[patch, rows, :].astype(jnp.float32)
            for tap in range(TAPS):
                part = moved(x_unit, tap // 3 - 1, tap % 3 - 1, masks)
                for half in range(PIX // 128):
                    taps_ref[half, pl.ds(unit * ROW + tap, CG, stride=TAPS), :] = part[
                        :, half * 128:(half + 1) * 128
                    ]
            grad = lax.dot_general(
                dy_all_ref[patch, rows, :],
                joined(taps_ref, unit * ROW, ROW).astype(jnp.bfloat16),
                (((1,), (1,)), ((), ())),
                preferred_element_type=jnp.float32,
            )
            put(grad_ref, unit * CG, grad)
        slots = []
        for place in range(together):
            patch = block * together + place
            column = tile * per_tile + lax.rem(patch, per_tile)
            slots.append([])
            for rank in range(top_count):
                expert = routes_ref[lax.div(patch, per_tile), rank, column]
                slots[-1].append(lax.div(expert, owned))
        for quad in range(CG // 4):
            parts = [None] * TAPS
            for j in range(4):
                line = rolled(strided(grad_ref, quad * 4 + j, rows_count, CG), 32 * j)
                for m in range(3):
                    piece = line[:, m * 128:(m + 1) * 128]
                    at = 2 * j + m
                    parts[at] = piece if parts[at] is None else parts[at] + piece
            flat = jnp.concatenate(parts, axis=1)
            for place in range(together):
                value = flat[place * groups:(place + 1) * groups].astype(jnp.bfloat16)
                lanes = slice(quad * QUAD, (quad + 1) * QUAD)
                grads_ref[block * together + place, :, lanes] = value
                for slot in slots[place]:
                    wire_ref[slot, :, lanes] = value
        return carry

    lax.fori_loop(0, samples * per_tile // together, work, 0)


def tables_kernel(owned, per_tile, routes_ref, logits_ref, local_ref, gate_ref):
    first = lax.axis_index("grid") * owned

    def scan(tile, carry):
        local, logit = jnp.int32(0), jnp.float32(0)
        for at, inside, hit in named(routes_ref, tile, per_tile, first, owned):
            local = jnp.where(hit, inside, local)
            logit = jnp.where(hit, logits_ref[at], logit)
        local_ref[tile] = local
        gate = jax.nn.sigmoid(jnp.full(gate_ref.shape[1:], logit, jnp.float32))
        gate_ref[tile] = gate / SIDE
        return carry

    lax.fori_loop(0, local_ref.shape[0], scan, 0)


def adjoint_unit(mixed_ref, spread_ref, unit, dy, masks):
    kernel = joined(mixed_ref, unit * CG, CG)[:, :ROW].astype(jnp.bfloat16)
    spread = lax.dot_general(
        kernel, dy, (((0,), (0,)), ((), ())), preferred_element_type=jnp.float32
    )
    put(spread_ref, unit * ROW, spread)
    total = jnp.zeros((CG, PIX), jnp.float32)
    for tap in range(TAPS):
        part = strided(spread_ref, unit * ROW + tap, CG, TAPS)
        total += moved(part, 1 - tap // 3, 1 - tap % 3, masks)
    return total.astype(jnp.bfloat16)


def adjoint_kernel(owned, routes_ref, logits_ref, grads_ref, dy_all_ref, *rest):
    pair_refs, rest = rest[:-9], rest[-9:]
    (
        out_ref, own_dots_ref, own_mixed_ref,
        kernels_ref, flat_ref, mixed_ref, spread_ref, dots_ref, place_sem,
    ) = rest
    samples, top_count, patches = routes_ref.shape
    tiles, groups, _ = kernels_ref.shape
    channels = groups * CG
    per_tile = patches // tiles
    together = min(ROWS // groups, per_tile)
    rows_count = together * groups
    per_sample = per_tile // together
    tile = lax.axis_index("grid")
    mine = lax.axis_index("batch")
    places = [
        (source.at[which], kernels_ref.at[tile ^ (2 * pair + which)])
        for pair, source in zip(pair_order(tiles), pair_refs)
        for which in range(2)
    ]
    copies = [
        pltpu.make_async_copy(source, target, place_sem.at[number])
        for number, (source, target) in enumerate(places)
    ]
    for copy in copies:
        copy.start()
    masks = pixel_masks(CG)
    for copy in copies:
        copy.wait()

    def mix(block, target_ref):
        for place in range(together):
            patch = block * together + place
            sample = lax.div(patch, per_tile)
            column = tile * per_tile + lax.rem(patch, per_tile)
            gates, slots = [], []
            for rank in range(top_count):
                logit = logits_ref[sample, rank, column]
                gates.append(jax.nn.sigmoid(jnp.full((groups, 128), logit, jnp.float32)))
                slots.append(lax.div(routes_ref[sample, rank, column], owned))
            dots = [jnp.zeros((groups, 128), jnp.float32) for _ in range(top_count)]
            for at in range(0, CG * ROW, 128):
                lanes = slice(at, at + 128)
                mixed = jnp.zeros((groups, 128), jnp.float32)
                grad = grads_ref[patch, :, lanes].astype(jnp.float32)
                for rank in range(top_count):
                    kernel = kernels_ref[slots[rank], :, lanes].astype(jnp.float32)
                    dots[rank] += kernel * grad
                    mixed += gates[rank] * kernel
                flat_ref[place * groups:(place + 1) * groups, lanes] = mixed
            for rank in range(top_count):
                start = (block * top_count + rank) * rows_count + place * groups
                dots_ref[pl.ds(start, groups), :] = dots[rank]
        for quad in range(CG // 4):
            for j in range(4):
                start = quad * QUAD + 2 * j * 128
                line = rolled(flat_ref[:, start:start + WIDE], -32 * j)
                for m in range(WIDE // 128):
                    target_ref[m, pl.ds(quad * 4 + j, rows_count, stride=CG), :] = line[
                        :, m * 128:(m + 1) * 128
                    ]

    def work(number, carry):
        step = 1 + lax.div(number, per_sample)
        within = lax.rem(number, per_sample)
        block = lax.rem(mine + step, samples) * per_sample + within
        mix(block, mixed_ref)
        for unit in range(rows_count):
            place = unit // groups
            rows = slice((unit % groups) * CG, (unit % groups + 1) * CG)
            dy = dy_all_ref[block * together + place, rows, :]
            offset = pl.multiple_of((within * together + place) * PIX, PIX)
            out_ref[step - 1, rows, pl.ds(offset, PIX)] = adjoint_unit(
                mixed_ref, spread_ref, unit, dy, masks
            )
        return carry

    def own(within, carry):
        mix(mine * per_sample + within, own_mixed_ref.at[within])
        return carry

    lax.fori_loop(0, (samples - 1) * per_sample, work, 0)
    lax.fori_loop(0, per_sample, own, 0)
    count = samples * per_sample * top_count * rows_count
    sums = lax.dot_general(
        jnp.ones((DOT_ROWS, 128), jnp.float32),
        dots_ref[...],
        (((1,), (1,)), ((), ())),
        precision=lax.Precision.HIGHEST,
        preferred_element_type=jnp.float32,
    )
    row = lax.broadcasted_iota(jnp.int32, (count, 128), 0)
    lane = lax.broadcasted_iota(jnp.int32, (count, 128), 1)
    row_patch = row // (top_count * rows_count) * together + row % rows_count // groups
    row_rank = row // rows_count % top_count
    chosen = (lane == row_patch * top_count + row_rank).astype(jnp.float32)
    route_dots = lax.dot_general(
        sums,
        chosen,
        (((1,), (0,)), ((), ())),
        precision=lax.Precision.HIGHEST,
        preferred_element_type=jnp.float32,
    ).astype(jnp.bfloat16)
    own_dots_ref[...] = route_dots
    for step in range(1, samples):
        out_ref[step - 1, channels:channels + DOT_ROWS, :128] = route_dots


def own_adjoint_kernel(mixed_ref, dy_all_ref, out_ref, spread_ref):
    per_sample, _, mixed_rows, _ = mixed_ref.shape
    rows_count = mixed_rows // CG
    channels, span = out_ref.shape
    groups = channels // CG
    together = rows_count // groups
    mine = lax.axis_index("batch")
    masks = pixel_masks(CG)

    def work(within, carry):
        for unit in range(rows_count):
            place = within * together + unit // groups
            rows = slice((unit % groups) * CG, (unit % groups + 1) * CG)
            dy = dy_all_ref[mine * (span // PIX) + place, rows, :]
            out_ref[rows, pl.ds(pl.multiple_of(place * PIX, PIX), PIX)] = adjoint_unit(
                mixed_ref.at[within], spread_ref, unit, dy, masks
            )
        return carry

    lax.fori_loop(0, per_sample, work, 0)


def sum_kernel(local_ref, gate_ref, got_ref, out_hbm, total_ref, sem):
    tiles, groups, width = got_ref.shape
    chunk = width // SUM_CHUNKS
    copies = []
    for part in range(SUM_CHUNKS):
        span = slice(part * chunk, (part + 1) * chunk)
        total_ref[:, :, span] = jnp.zeros(total_ref.shape[:2] + (chunk,), jnp.float32)

        def add(quad, carry):
            for tile in (quad * 4 + i for i in range(4)):
                local = local_ref[tile]
                gate = gate_ref[tile]
                for at in range(part * chunk, (part + 1) * chunk, 128):
                    lanes = slice(at, at + 128)
                    total_ref[local, :, lanes] += gate * got_ref[tile, :, lanes].astype(jnp.float32)
            return carry

        lax.fori_loop(0, tiles // 4, add, 0)
        copies.append(
            pltpu.make_async_copy(total_ref.at[:, :, span], out_hbm.at[:, :, span], sem.at[part])
        )
        copies[-1].start()
    for copy in copies:
        copy.wait()


def per_device(inputs, cotangent, weights, gate_logits, routes):
    tiles = lax.axis_size("grid")
    batch = lax.axis_size("batch")
    owned, groups, width = weights.shape
    samples, patches, top_count = routes.shape
    per_tile = patches // tiles
    span = inputs.shape[2]
    channels = groups * CG
    assert samples * per_tile * top_count == tiles and samples == batch
    smem = pl.BlockSpec(memory_space=pltpu.SMEM)
    vmem = pl.BlockSpec(memory_space=pltpu.VMEM)
    hbm = pl.BlockSpec(memory_space=pltpu.HBM)
    anywhere = pl.BlockSpec(memory_space=pl.ANY)
    params = pltpu.CompilerParams(vmem_limit_bytes=VMEM_LIMIT)
    routes_t = routes.transpose(0, 2, 1)
    logits_t = gate_logits.transpose(0, 2, 1)
    assert tiles & (tiles - 1) == 0 and tiles >= 4
    together = min(ROWS // groups, per_tile)
    rows = together * groups

    def blocks_shape(count):
        return jax.ShapeDtypeStruct((count, groups, width), jnp.bfloat16)

    def swap(blocks, step):
        return lax.ppermute(blocks, "grid", [(i, i ^ step) for i in range(tiles)])

    weights_beside = swap(weights, 1)
    pair_count = tiles // 2
    table = jax.ShapeDtypeStruct((pair_count,), jnp.int32)
    own_ids, beside_ids = pl.pallas_call(
        functools.partial(scan_kernel, owned, per_tile),
        out_shape=(table, table),
        in_specs=[smem],
        out_specs=(smem, smem),
        compiler_params=params,
        cost_estimate=pl.CostEstimate(flops=COST, bytes_accessed=1, transcendentals=0),
        name="scan",
    )(routes_t)

    to_send, *pairs = pl.pallas_call(
        pack_kernel,
        out_shape=(jax.ShapeDtypeStruct((batch - 1, 2, channels, span), jnp.bfloat16),)
        + (blocks_shape(2),) * pair_count,
        in_specs=[smem, smem] + [vmem] * 4,
        out_specs=(hbm,) * (1 + pair_count),
        scratch_shapes=[
            pltpu.SemaphoreType.DMA((pair_count, 2)),
            pltpu.SemaphoreType.DMA((batch - 1, 2)),
        ],
        compiler_params=params,
        name="pack",
    )(own_ids, beside_ids, weights, weights_beside, inputs, cotangent)
    pairs = [
        blocks if pair == 0 else swap(blocks, 2 * pair)
        for pair, blocks in zip(pair_order(tiles), pairs)
    ]

    def exchange(blocks):
        return [
            lax.ppermute(
                blocks[step - 1], "batch", [(i, (i + step) % batch) for i in range(batch)]
            )
            for step in range(1, batch)
        ]

    got = jnp.stack(exchange([to_send[step] for step in range(batch - 1)]))

    work = samples * patches // tiles * groups * width * PIX * 2
    wire, grads, dy_all = pl.pallas_call(
        functools.partial(grads_kernel, owned),
        out_shape=(
            blocks_shape(tiles),
            blocks_shape(samples * per_tile),
            jax.ShapeDtypeStruct((samples * per_tile, channels, PIX), jnp.bfloat16),
        ),
        in_specs=[smem, vmem, vmem, vmem],
        out_specs=(vmem, vmem, vmem),
        scratch_shapes=[
            pltpu.VMEM((samples * per_tile, channels, PIX), jnp.bfloat16),
            pltpu.VMEM((PIX // 128, rows * ROW, 128), jnp.float32),
            pltpu.VMEM((WIDE // 128, rows * CG, 128), jnp.float32),
        ],
        compiler_params=params,
        cost_estimate=pl.CostEstimate(flops=COST, bytes_accessed=1, transcendentals=0),
        name="kernel_grads",
    )(routes_t, inputs, cotangent, got)

    grads_back = lax.all_to_all(wire, "grid", split_axis=0, concat_axis=0, tiled=True)

    per_sample = per_tile // together
    parts, own_dots, own_mixed = pl.pallas_call(
        functools.partial(adjoint_kernel, owned),
        out_shape=(
            jax.ShapeDtypeStruct((batch - 1, channels + DOT_ROWS, span), jnp.bfloat16),
            jax.ShapeDtypeStruct((DOT_ROWS, 128), jnp.bfloat16),
            jax.ShapeDtypeStruct((per_sample, WIDE // 128, rows * CG, 128), jnp.float32),
        ),
        in_specs=[smem, smem, vmem, vmem] + [anywhere] * (tiles // 2),
        out_specs=(vmem, vmem, vmem),
        scratch_shapes=[
            pltpu.VMEM((tiles, groups, width), jnp.bfloat16),
            pltpu.VMEM((rows, width), jnp.float32),
            pltpu.VMEM((WIDE // 128, rows * CG, 128), jnp.float32),
            pltpu.VMEM((PIX // 128, rows * ROW, 128), jnp.float32),
            pltpu.VMEM((samples * per_tile * top_count * groups, 128), jnp.float32),
            pltpu.SemaphoreType.DMA((tiles,)),
        ],
        compiler_params=params,
        cost_estimate=pl.CostEstimate(flops=COST, bytes_accessed=1, transcendentals=0),
        name="adjoint",
    )(routes_t, logits_t, grads, dy_all, *pairs)

    own_part = pl.pallas_call(
        own_adjoint_kernel,
        out_shape=jax.ShapeDtypeStruct((channels, span), jnp.bfloat16),
        in_specs=[vmem, vmem],
        out_specs=vmem,
        scratch_shapes=[pltpu.VMEM((PIX // 128, rows * ROW, 128), jnp.float32)],
        compiler_params=params,
        cost_estimate=pl.CostEstimate(flops=COST // 20, bytes_accessed=1, transcendentals=0),
        name="own_adjoint",
    )(own_mixed, dy_all)

    late_routes, late_logits, _ = lax.optimization_barrier((routes_t, logits_t, own_dots))
    local, gate_table = pl.pallas_call(
        functools.partial(tables_kernel, owned, per_tile),
        out_shape=(
            jax.ShapeDtypeStruct((tiles,), jnp.int32),
            jax.ShapeDtypeStruct((tiles, groups, 128), jnp.float32),
        ),
        in_specs=[smem, smem],
        out_specs=(smem, vmem),
        compiler_params=params,
        name="tables",
    )(late_routes, late_logits)

    arrived = exchange([parts[step] for step in range(batch - 1)])
    mine = lax.axis_index("batch")
    d_inputs = jnp.zeros(inputs.shape, jnp.bfloat16)
    dots = own_dots[0].astype(jnp.float32)
    for step, part in enumerate([own_part] + arrived):
        block = lax.rem(mine - step + batch, batch)
        d_inputs = lax.dynamic_update_slice(
            d_inputs, part[None, :channels], (0, block * channels, 0)
        )
        if step:
            dots += part[channels, :128].astype(jnp.float32)
    dots = dots[:tiles].reshape(samples, per_tile, top_count)
    gates = jax.nn.sigmoid(
        lax.dynamic_slice_in_dim(gate_logits, lax.axis_index("grid") * per_tile, per_tile, 1)
    )
    gate_grad = gates * (1.0 - gates) * dots / SIDE

    d_weights = pl.pallas_call(
        sum_kernel,
        out_shape=jax.ShapeDtypeStruct(weights.shape, jnp.float32),
        in_specs=[smem, vmem, vmem],
        out_specs=hbm,
        scratch_shapes=[
            pltpu.VMEM(weights.shape, jnp.float32),
            pltpu.SemaphoreType.DMA((SUM_CHUNKS,)),
        ],
        compiler_params=params,
        name="weight_sum",
    )(local, gate_table, grads_back)
    return (d_inputs, d_weights, gate_grad)


def solution(mesh):
    placed = (
        P("batch", None, "grid"),
        P("batch", None, "grid"),
        P("grid", "batch", None),
        P(),
        P(),
    )
    return jax.shard_map(
        per_device,
        mesh=mesh,
        in_specs=placed,
        out_specs=(P("batch", None, "grid"), P("grid", "batch", None), P(None, "grid", None)),
        check_vma=False,
    )
```

```python
import functools

import jax
import jax.numpy as jnp
from jax import lax
from jax.experimental import pallas as pl
from jax.experimental.pallas import tpu as pltpu
from jax.sharding import PartitionSpec as P

CG = 32
SIDE = 16
PIX = SIDE * SIDE
TAPS = 9
ROW = CG * TAPS
WIDE = 384
QUAD = 4 * ROW
ROWS = 8
DOT_ROWS = 16
VMEM_LIMIT = 16 * 1024 * 1024
WHOLE_VMEM = 60 * 1024 * 1024
EARLY = 3
SUM_CHUNKS = 3
COST = 20_000_000_000


def rolled(values, shift):
    extent = values.shape[1]
    shift %= extent
    return values if shift == 0 else pltpu.roll(values, shift, 1)


def pixel_masks(rows):
    pixel = lax.broadcasted_iota(jnp.int32, (rows, PIX), 1)
    column = pixel % SIDE
    return {
        "row": {-1: pixel >= SIDE, 1: pixel < PIX - SIDE},
        "column": {-1: column > 0, 1: column < SIDE - 1},
    }


def moved(values, row_shift, column_shift, masks):
    out = rolled(values, -(row_shift * SIDE + column_shift))
    if row_shift:
        out = jnp.where(masks["row"][row_shift], out, 0.0)
    if column_shift:
        out = jnp.where(masks["column"][column_shift], out, 0.0)
    return out


def joined(ref, start, count):
    return jnp.concatenate([ref[m, start:start + count, :] for m in range(ref.shape[0])], axis=1)


def strided(ref, start, count, stride):
    return jnp.concatenate(
        [ref[m, pl.ds(start, count, stride=stride), :] for m in range(ref.shape[0])], axis=1
    )


def put(ref, start, values):
    for at in range(0, values.shape[1], 128):
        piece = values[:, at:at + 128]
        ref[at // 128, start:start + values.shape[0], :piece.shape[1]] = piece


def pair_order(tiles):
    near, far = list(range(tiles // 4)), list(range(tiles // 4, tiles // 2))
    first = far.pop(len(far) // 2)
    return near[1:2] + [first] + near[2:] + far + near[:1]


def tree_sum(values):
    while len(values) > 1:
        values = [sum(values[at:at + 2]) for at in range(0, len(values), 2)]
    return values[0]


def stage_kernel(x_hbm, dy_hbm, send_ref, halves_ref, halves_sem, send_sem):
    others, _, channels, _ = send_ref.shape
    mine = lax.axis_index("batch")
    taken, sent = [], []
    for step in range(1, others + 1):
        block = lax.rem(mine + step, others + 1)
        rows = pl.ds(pl.multiple_of(block * channels, channels), channels)
        for which, source in enumerate((x_hbm, dy_hbm)):
            at = (step - 1, which)
            taken.append(
                pltpu.make_async_copy(source.at[0, rows], halves_ref.at[at], halves_sem.at[at])
            )
            sent.append(
                pltpu.make_async_copy(halves_ref.at[at], send_ref.at[at], send_sem.at[at])
            )
    for copy in taken:
        copy.start()
    for copy, then in zip(taken, sent):
        copy.wait()
        then.start()
    for copy in sent:
        copy.wait()


def pack_kernel(owned, per_tile, pairs, routes_ref, own_ref, beside_ref, *rest):
    pair_refs, sem = rest[:-1], rest[-1]
    samples, top_count, _ = routes_ref.shape
    here = lax.axis_index("grid")
    copies = []
    for pair, target in zip(pairs, pair_refs):
        column = (here ^ (2 * pair)) * per_tile
        experts = [
            routes_ref[sample, rank, column + place]
            for sample in range(samples)
            for rank in range(top_count)
            for place in range(per_tile)
        ]
        for which, source in enumerate((own_ref, beside_ref)):
            inside = [expert - (here ^ which) * owned for expert in experts]
            found = tree_sum([jnp.where((at >= 0) & (at < owned), at, 0) for at in inside])
            copies.append(
                pltpu.make_async_copy(source.at[found], target.at[which], sem.at[pair, which])
            )
            copies[-1].start()
    for copy in copies:
        copy.wait()


def unit_grad(x, dy, unit, taps_ref, grad_ref, masks):
    x = x.astype(jnp.float32)
    for tap in range(TAPS):
        part = moved(x, tap // 3 - 1, tap % 3 - 1, masks)
        for half in range(PIX // 128):
            taps_ref[half, pl.ds(unit * ROW + tap, CG, stride=TAPS), :] = part[
                :, half * 128:(half + 1) * 128
            ]
    grad = lax.dot_general(
        dy,
        joined(taps_ref, unit * ROW, ROW).astype(jnp.bfloat16),
        (((1,), (1,)), ((), ())),
        preferred_element_type=jnp.float32,
    )
    put(grad_ref, unit * CG, grad)


def flat_quads(grad_ref, rows_count):
    for quad in range(CG // 4):
        parts = [None] * TAPS
        for j in range(4):
            line = rolled(strided(grad_ref, quad * 4 + j, rows_count, CG), 32 * j)
            for m in range(3):
                piece = line[:, m * 128:(m + 1) * 128]
                at = 2 * j + m
                parts[at] = piece if parts[at] is None else parts[at] + piece
        flat = jnp.concatenate(parts, axis=1).astype(jnp.bfloat16)
        yield slice(quad * QUAD, (quad + 1) * QUAD), flat


def grads_kernel(owned, per_tile, routes_ref, x_ref, dy_ref, got_ref, wire_ref, taps_ref, grad_ref):
    samples, top_count, _ = routes_ref.shape
    groups = wire_ref.shape[1]
    together = min(ROWS // groups, per_tile)
    rows_count = together * groups
    per_sample = per_tile // together
    tile = lax.axis_index("grid")
    mine = lax.axis_index("batch")
    grad_ref[WIDE // 128 - 1] = jnp.zeros((rows_count * CG, 128), jnp.float32)
    masks = pixel_masks(CG)

    def work(sample, block, read):
        for unit in range(rows_count):
            place = block * together + unit // groups
            span = pl.ds(pl.multiple_of(place * PIX, PIX), PIX)
            x, dy = read(unit % groups, span)
            unit_grad(x, dy, unit, taps_ref, grad_ref, masks)
        slots = []
        for place in range(together):
            column = tile * per_tile + block * together + place
            slots.append(
                [lax.div(routes_ref[sample, rank, column], owned) for rank in range(top_count)]
            )
        for lanes, flat in flat_quads(grad_ref, rows_count):
            for place in range(together):
                for slot in slots[place]:
                    wire_ref[slot, :, lanes] = flat[place * groups:(place + 1) * groups]

    def own(block, carry):
        def read(group, span):
            row = pl.multiple_of((mine * groups + group) * CG, CG)
            return tuple(ref[0, pl.ds(row, CG), span] for ref in (x_ref, dy_ref))

        work(mine, block, read)
        return carry

    def other(number, carry):
        step = lax.div(number, per_sample)

        def read(group, span):
            rows = slice(group * CG, (group + 1) * CG)
            return tuple(got_ref[step, which, rows, span] for which in range(2))

        work(lax.rem(mine - step - 1 + samples, samples), lax.rem(number, per_sample), read)
        return carry

    lax.fori_loop(0, per_sample, own, 0)
    lax.fori_loop(0, (samples - 1) * per_sample, other, 0)


def tables_kernel(owned, per_tile, routes_ref, logits_ref, local_ref, gate_ref):
    samples, top_count, _ = routes_ref.shape
    first = lax.axis_index("grid") * owned

    def scan(tile, carry):
        locals_hit, logits_hit = [], []
        for sample in range(samples):
            for rank in range(top_count):
                for place in range(per_tile):
                    at = (sample, rank, tile * per_tile + place)
                    inside = routes_ref[at] - first
                    hit = (inside >= 0) & (inside < owned)
                    locals_hit.append(jnp.where(hit, inside, 0))
                    logits_hit.append(jnp.where(hit, logits_ref[at], 0.0))
        local_ref[tile] = tree_sum(locals_hit)
        gate = jax.nn.sigmoid(jnp.full(gate_ref.shape[1:], tree_sum(logits_hit), jnp.float32))
        gate_ref[tile] = gate / SIDE
        return carry

    lax.fori_loop(0, local_ref.shape[0], scan, 0)


def adjoint_unit(mixed_ref, spread_ref, unit, dy, masks):
    kernel = joined(mixed_ref, unit * CG, CG)[:, :ROW].astype(jnp.bfloat16)
    spread = lax.dot_general(
        kernel, dy, (((0,), (0,)), ((), ())), preferred_element_type=jnp.float32
    )
    put(spread_ref, unit * ROW, spread)
    total = jnp.zeros((CG, PIX), jnp.float32)
    for tap in range(TAPS):
        part = strided(spread_ref, unit * ROW + tap, CG, TAPS)
        total += moved(part, 1 - tap // 3, 1 - tap % 3, masks)
    return total.astype(jnp.bfloat16)


def adjoint_kernel(owned, routes_ref, logits_ref, wire_ref, got_ref, *rest):
    pair_refs, rest = rest[:-12], rest[-12:]
    (
        out_ref, own_dots_ref, own_mixed_ref,
        grads_ref, dy_ref, kernels_ref, flat_ref, mixed_ref, spread_ref, dots_ref, place_sem,
        fetch_sem,
    ) = rest
    samples, top_count, patches = routes_ref.shape
    tiles, groups, _ = kernels_ref.shape
    channels = groups * CG
    per_tile = patches // tiles
    together = min(ROWS // groups, per_tile)
    rows_count = together * groups
    per_sample = per_tile // together
    tile = lax.axis_index("grid")
    mine = lax.axis_index("batch")
    places = [
        (source.at[which], kernels_ref.at[tile ^ (2 * pair + which)])
        for pair, source in zip(pair_order(tiles), pair_refs)
        for which in range(2)
    ]
    copies = [
        pltpu.make_async_copy(source, target, place_sem.at[number])
        for number, (source, target) in enumerate(places)
    ]
    copies.append(pltpu.make_async_copy(wire_ref, grads_ref, fetch_sem.at[0]))
    copies.append(pltpu.make_async_copy(got_ref.at[:, 1], dy_ref, fetch_sem.at[1]))
    for copy in copies:
        copy.start()
    masks = pixel_masks(CG)
    for copy in copies:
        copy.wait()

    def mix(block, target_ref):
        for place in range(together):
            patch = block * together + place
            sample = lax.div(patch, per_tile)
            column = tile * per_tile + lax.rem(patch, per_tile)
            gates, slots = [], []
            for rank in range(top_count):
                logit = logits_ref[sample, rank, column]
                gates.append(jax.nn.sigmoid(jnp.full((groups, 128), logit, jnp.float32)))
                slots.append(lax.div(routes_ref[sample, rank, column], owned))
            dots = [jnp.zeros((groups, 128), jnp.float32) for _ in range(top_count)]
            for at in range(0, CG * ROW, 128):
                lanes = slice(at, at + 128)
                mixed = jnp.zeros((groups, 128), jnp.float32)
                grad = grads_ref[slots[0], :, lanes].astype(jnp.float32)
                for rank in range(top_count):
                    kernel = kernels_ref[slots[rank], :, lanes].astype(jnp.float32)
                    dots[rank] += kernel * grad
                    mixed += gates[rank] * kernel
                flat_ref[place * groups:(place + 1) * groups, lanes] = mixed
            for rank in range(top_count):
                start = (block * top_count + rank) * rows_count + place * groups
                dots_ref[pl.ds(start, groups), :] = dots[rank]
        for quad in range(CG // 4):
            for j in range(4):
                start = quad * QUAD + 2 * j * 128
                line = rolled(flat_ref[:, start:start + WIDE], -32 * j)
                for m in range(WIDE // 128):
                    target_ref[m, pl.ds(quad * 4 + j, rows_count, stride=CG), :] = line[
                        :, m * 128:(m + 1) * 128
                    ]

    def work(number, carry):
        step = 1 + lax.div(number, per_sample)
        within = lax.rem(number, per_sample)
        block = lax.rem(mine + step, samples) * per_sample + within
        mix(block, mixed_ref)
        for unit in range(rows_count):
            place = unit // groups
            rows = slice((unit % groups) * CG, (unit % groups + 1) * CG)
            span = pl.ds(pl.multiple_of((within * together + place) * PIX, PIX), PIX)
            dy = dy_ref[samples - 1 - step, rows, span]
            out_ref[step - 1, rows, span] = adjoint_unit(
                mixed_ref, spread_ref, unit, dy, masks
            )
        return carry

    def own(within, carry):
        mix(mine * per_sample + within, own_mixed_ref.at[within])
        return carry

    lax.fori_loop(0, (samples - 1) * per_sample, work, 0)
    lax.fori_loop(0, per_sample, own, 0)
    count = samples * per_sample * top_count * rows_count
    sums = lax.dot_general(
        jnp.ones((DOT_ROWS, 128), jnp.float32),
        dots_ref[...],
        (((1,), (1,)), ((), ())),
        precision=lax.Precision.HIGHEST,
        preferred_element_type=jnp.float32,
    )
    row = lax.broadcasted_iota(jnp.int32, (count, 128), 0)
    lane = lax.broadcasted_iota(jnp.int32, (count, 128), 1)
    row_patch = row // (top_count * rows_count) * together + row % rows_count // groups
    row_rank = row // rows_count % top_count
    chosen = (lane == row_patch * top_count + row_rank).astype(jnp.float32)
    route_dots = lax.dot_general(
        sums,
        chosen,
        (((1,), (0,)), ((), ())),
        precision=lax.Precision.HIGHEST,
        preferred_element_type=jnp.float32,
    ).astype(jnp.bfloat16)
    own_dots_ref[...] = route_dots
    for step in range(1, samples):
        out_ref[step - 1, channels:channels + DOT_ROWS, :128] = route_dots


def own_adjoint_kernel(mixed_ref, dy_ref, out_ref, spread_ref):
    per_sample, _, mixed_rows, _ = mixed_ref.shape
    rows_count = mixed_rows // CG
    groups = out_ref.shape[0] // CG
    together = rows_count // groups
    mine = lax.axis_index("batch")
    masks = pixel_masks(CG)

    def work(within, carry):
        for unit in range(rows_count):
            place = within * together + unit // groups
            group = unit % groups
            lanes = pl.ds(pl.multiple_of(place * PIX, PIX), PIX)
            row = pl.multiple_of((mine * groups + group) * CG, CG)
            out_ref[group * CG:(group + 1) * CG, lanes] = adjoint_unit(
                mixed_ref.at[within], spread_ref, unit, dy_ref[0, pl.ds(row, CG), lanes], masks
            )
        return carry

    lax.fori_loop(0, per_sample, work, 0)


def sum_kernel(local_ref, gate_ref, got_ref, out_hbm, total_ref, sem):
    tiles, groups, width = got_ref.shape
    chunk = width // SUM_CHUNKS
    copies = []
    for part in range(SUM_CHUNKS):
        span = slice(part * chunk, (part + 1) * chunk)
        total_ref[:, :, span] = jnp.zeros(total_ref.shape[:2] + (chunk,), jnp.float32)

        def add(quad, carry):
            for tile in (quad * 4 + i for i in range(4)):
                local = local_ref[tile]
                gate = gate_ref[tile]
                for at in range(part * chunk, (part + 1) * chunk, 128):
                    lanes = slice(at, at + 128)
                    total_ref[local, :, lanes] += gate * got_ref[tile, :, lanes].astype(jnp.float32)
            return carry

        lax.fori_loop(0, tiles // 4, add, 0)
        copies.append(
            pltpu.make_async_copy(total_ref.at[:, :, span], out_hbm.at[:, :, span], sem.at[part])
        )
        copies[-1].start()
    for copy in copies:
        copy.wait()


def per_device(inputs, cotangent, weights, gate_logits, routes):
    tiles = lax.axis_size("grid")
    batch = lax.axis_size("batch")
    owned, groups, width = weights.shape
    samples, patches, top_count = routes.shape
    per_tile = patches // tiles
    span = inputs.shape[2]
    channels = groups * CG
    assert samples * per_tile * top_count == tiles and samples == batch
    smem = pl.BlockSpec(memory_space=pltpu.SMEM)
    vmem = pl.BlockSpec(memory_space=pltpu.VMEM)
    hbm = pl.BlockSpec(memory_space=pltpu.HBM)
    anywhere = pl.BlockSpec(memory_space=pl.ANY)
    params = pltpu.CompilerParams(vmem_limit_bytes=VMEM_LIMIT)
    routes_t = routes.transpose(0, 2, 1)
    logits_t = gate_logits.transpose(0, 2, 1)
    assert tiles & (tiles - 1) == 0 and tiles >= 4
    together = min(ROWS // groups, per_tile)
    rows = together * groups

    def blocks_shape(count):
        return jax.ShapeDtypeStruct((count, groups, width), jnp.bfloat16)

    def swap(blocks, step):
        return lax.ppermute(blocks, "grid", [(i, i ^ step) for i in range(tiles)])

    weights_beside = swap(weights, 1)
    pair_count = tiles // 2
    pairs = []
    order = pair_order(tiles)
    for some in (order[:EARLY], order[EARLY:]):
        pairs += pl.pallas_call(
            functools.partial(pack_kernel, owned, per_tile, some),
            out_shape=(blocks_shape(2),) * len(some),
            in_specs=[smem, vmem, vmem],
            out_specs=(hbm,) * len(some),
            scratch_shapes=[pltpu.SemaphoreType.DMA((pair_count, 2))],
            compiler_params=params,
            name="pack",
        )(routes_t, weights, weights_beside)
    pairs = [
        blocks if pair == 0 else swap(blocks, 2 * pair)
        for pair, blocks in zip(pair_order(tiles), pairs)
    ]

    def exchange(blocks):
        return [
            lax.ppermute(
                blocks[step - 1], "batch", [(i, (i + step) % batch) for i in range(batch)]
            )
            for step in range(1, batch)
        ]

    mine = lax.axis_index("batch")
    to_send = pl.pallas_call(
        stage_kernel,
        out_shape=jax.ShapeDtypeStruct((batch - 1, 2, channels, span), jnp.bfloat16),
        in_specs=[hbm] * 2,
        out_specs=hbm,
        scratch_shapes=[
            pltpu.VMEM((batch - 1, 2, channels, span), jnp.bfloat16),
            pltpu.SemaphoreType.DMA((batch - 1, 2)),
            pltpu.SemaphoreType.DMA((batch - 1, 2)),
        ],
        compiler_params=pltpu.CompilerParams(vmem_limit_bytes=WHOLE_VMEM),
        cost_estimate=pl.CostEstimate(flops=COST, bytes_accessed=1, transcendentals=0),
        name="stage",
    )(inputs, cotangent)
    got = jnp.stack(exchange([to_send[step] for step in range(batch - 1)]))

    grad_scratch = [
        pltpu.VMEM((PIX // 128, rows * ROW, 128), jnp.float32),
        pltpu.VMEM((WIDE // 128, rows * CG, 128), jnp.float32),
    ]
    wire = pl.pallas_call(
        functools.partial(grads_kernel, owned, per_tile),
        out_shape=blocks_shape(tiles),
        in_specs=[smem, vmem, vmem, vmem],
        out_specs=vmem,
        scratch_shapes=grad_scratch,
        compiler_params=params,
        cost_estimate=pl.CostEstimate(flops=COST, bytes_accessed=1, transcendentals=0),
        name="kernel_grads",
    )(routes_t, inputs, cotangent, got)

    wire, _ = lax.optimization_barrier((wire, pairs[:2]))
    grads_back = lax.all_to_all(wire, "grid", split_axis=0, concat_axis=0, tiled=True)

    per_sample = per_tile // together
    parts, own_dots, own_mixed = pl.pallas_call(
        functools.partial(adjoint_kernel, owned),
        out_shape=(
            jax.ShapeDtypeStruct((batch - 1, channels + DOT_ROWS, span), jnp.bfloat16),
            jax.ShapeDtypeStruct((DOT_ROWS, 128), jnp.bfloat16),
            jax.ShapeDtypeStruct((per_sample, WIDE // 128, rows * CG, 128), jnp.float32),
        ),
        in_specs=[smem, smem] + [anywhere] * (2 + pair_count),
        out_specs=(vmem, vmem, vmem),
        scratch_shapes=[
            pltpu.VMEM((tiles, groups, width), jnp.bfloat16),
            pltpu.VMEM((batch - 1, channels, span), jnp.bfloat16),
            pltpu.VMEM((tiles, groups, width), jnp.bfloat16),
            pltpu.VMEM((rows, width), jnp.float32),
            pltpu.VMEM((WIDE // 128, rows * CG, 128), jnp.float32),
            pltpu.VMEM((PIX // 128, rows * ROW, 128), jnp.float32),
            pltpu.VMEM((samples * per_tile * top_count * groups, 128), jnp.float32),
            pltpu.SemaphoreType.DMA((tiles,)),
            pltpu.SemaphoreType.DMA((2,)),
        ],
        compiler_params=params,
        cost_estimate=pl.CostEstimate(flops=COST, bytes_accessed=1, transcendentals=0),
        name="adjoint",
    )(routes_t, logits_t, wire, got, *pairs)

    own_part = pl.pallas_call(
        own_adjoint_kernel,
        out_shape=jax.ShapeDtypeStruct((channels, span), jnp.bfloat16),
        in_specs=[vmem, vmem],
        out_specs=vmem,
        scratch_shapes=[pltpu.VMEM((PIX // 128, rows * ROW, 128), jnp.float32)],
        compiler_params=params,
        cost_estimate=pl.CostEstimate(flops=COST // 20, bytes_accessed=1, transcendentals=0),
        name="own_adjoint",
    )(own_mixed, cotangent)

    late_routes, late_logits, _ = lax.optimization_barrier((routes_t, logits_t, own_dots))
    local, gate_table = pl.pallas_call(
        functools.partial(tables_kernel, owned, per_tile),
        out_shape=(
            jax.ShapeDtypeStruct((tiles,), jnp.int32),
            jax.ShapeDtypeStruct((tiles, groups, 128), jnp.float32),
        ),
        in_specs=[smem, smem],
        out_specs=(smem, vmem),
        compiler_params=params,
        name="tables",
    )(late_routes, late_logits)

    arrived = exchange([parts[step] for step in range(batch - 1)])
    d_inputs = jnp.zeros(inputs.shape, jnp.bfloat16)
    dots = own_dots[0].astype(jnp.float32)
    for step, part in enumerate([own_part] + arrived):
        block = lax.rem(mine - step + batch, batch)
        d_inputs = lax.dynamic_update_slice(
            d_inputs, part[None, :channels], (0, block * channels, 0)
        )
        if step:
            dots += part[channels, :128].astype(jnp.float32)
    dots = dots[:tiles].reshape(samples, per_tile, top_count)
    gates = jax.nn.sigmoid(
        lax.dynamic_slice_in_dim(late_logits, lax.axis_index("grid") * per_tile, per_tile, 2)
    ).transpose(0, 2, 1)
    gate_grad = gates * (1.0 - gates) * dots / SIDE

    d_weights = pl.pallas_call(
        sum_kernel,
        out_shape=jax.ShapeDtypeStruct(weights.shape, jnp.float32),
        in_specs=[smem, vmem, vmem],
        out_specs=hbm,
        scratch_shapes=[
            pltpu.VMEM(weights.shape, jnp.float32),
            pltpu.SemaphoreType.DMA((SUM_CHUNKS,)),
        ],
        compiler_params=params,
        name="weight_sum",
    )(local, gate_table, grads_back)
    return (d_inputs, d_weights, gate_grad)


def solution(mesh):
    placed = (
        P("batch", None, "grid"),
        P("batch", None, "grid"),
        P("grid", "batch", None),
        P(),
        P(),
    )
    return jax.shard_map(
        per_device,
        mesh=mesh,
        in_specs=placed,
        out_specs=(P("batch", None, "grid"), P("grid", "batch", None), P(None, "grid", None)),
        check_vma=False,
    )
```

```python
import functools

import jax
import jax.numpy as jnp
from jax import lax
from jax.experimental import pallas as pl
from jax.experimental.pallas import tpu as pltpu
from jax.sharding import PartitionSpec as P

CG = 32
SIDE = 16
PIX = SIDE * SIDE
TAPS = 9
ROW = CG * TAPS
WIDE = 384
QUAD = 4 * ROW
ROWS = 8
DOT_ROWS = 16
VMEM_LIMIT = 16 * 1024 * 1024
WHOLE_VMEM = 60 * 1024 * 1024
EARLY = 3
SUM_CHUNKS = 3
COST = 20_000_000_000


def rolled(values, shift):
    extent = values.shape[1]
    shift %= extent
    return values if shift == 0 else pltpu.roll(values, shift, 1)


def pixel_masks(rows):
    pixel = lax.broadcasted_iota(jnp.int32, (rows, PIX), 1)
    column = pixel % SIDE
    in_row = {-1: pixel >= SIDE, 0: None, 1: pixel < PIX - SIDE}
    in_column = {-1: column > 0, 0: None, 1: column < SIDE - 1}
    masks = {}
    for row_shift, row_mask in in_row.items():
        for column_shift, column_mask in in_column.items():
            both = [mask for mask in (row_mask, column_mask) if mask is not None]
            masks[row_shift, column_shift] = both[0] & both[-1] if both else None
    return masks


def moved(values, row_shift, column_shift, masks):
    out = rolled(values, -(row_shift * SIDE + column_shift))
    mask = masks[row_shift, column_shift]
    return out if mask is None else jnp.where(mask, out, 0.0)


def joined(ref, start, count):
    return jnp.concatenate([ref[m, start:start + count, :] for m in range(ref.shape[0])], axis=1)


def strided(ref, start, count, stride):
    return jnp.concatenate(
        [ref[m, pl.ds(start, count, stride=stride), :] for m in range(ref.shape[0])], axis=1
    )


def put(ref, start, values):
    for at in range(0, values.shape[1], 128):
        piece = values[:, at:at + 128]
        ref[at // 128, start:start + values.shape[0], :piece.shape[1]] = piece


def pair_order(tiles):
    near, far = list(range(tiles // 4)), list(range(tiles // 4, tiles // 2))
    first = far.pop(len(far) // 2)
    return near[1:2] + [first] + near[2:] + far + near[:1]


def tree_sum(values):
    while len(values) > 1:
        values = [sum(values[at:at + 2]) for at in range(0, len(values), 2)]
    return values[0]


def stage_kernel(x_hbm, dy_hbm, send_ref, halves_ref, halves_sem, send_sem):
    others, _, channels, _ = send_ref.shape
    mine = lax.axis_index("batch")
    taken, sent = [], []
    for step in range(1, others + 1):
        block = lax.rem(mine + step, others + 1)
        rows = pl.ds(pl.multiple_of(block * channels, channels), channels)
        for which, source in enumerate((x_hbm, dy_hbm)):
            at = (step - 1, which)
            taken.append(
                pltpu.make_async_copy(source.at[0, rows], halves_ref.at[at], halves_sem.at[at])
            )
            sent.append(
                pltpu.make_async_copy(halves_ref.at[at], send_ref.at[at], send_sem.at[at])
            )
    for copy in taken:
        copy.start()
    for copy, then in zip(taken, sent):
        copy.wait()
        then.start()
    for copy in sent:
        copy.wait()


def pack_kernel(owned, per_tile, pairs, routes_ref, own_ref, beside_ref, *rest):
    pair_refs, sem = rest[:-1], rest[-1]
    samples, top_count, _ = routes_ref.shape
    here = lax.axis_index("grid")
    copies = []
    for pair, target in zip(pairs, pair_refs):
        column = (here ^ (2 * pair)) * per_tile
        experts = [
            routes_ref[sample, rank, column + place]
            for sample in range(samples)
            for rank in range(top_count)
            for place in range(per_tile)
        ]
        for which, source in enumerate((own_ref, beside_ref)):
            inside = [expert - (here ^ which) * owned for expert in experts]
            found = tree_sum([jnp.where((at >= 0) & (at < owned), at, 0) for at in inside])
            copies.append(
                pltpu.make_async_copy(source.at[found], target.at[which], sem.at[pair, which])
            )
            copies[-1].start()
    for copy in copies:
        copy.wait()


def unit_grad(x, dy, unit, taps_ref, grad_ref, masks):
    x = x.astype(jnp.float32)
    for tap in range(TAPS):
        part = moved(x, tap // 3 - 1, tap % 3 - 1, masks)
        for half in range(PIX // 128):
            taps_ref[half, pl.ds(unit * ROW + tap, CG, stride=TAPS), :] = part[
                :, half * 128:(half + 1) * 128
            ]
    grad = lax.dot_general(
        dy,
        joined(taps_ref, unit * ROW, ROW).astype(jnp.bfloat16),
        (((1,), (1,)), ((), ())),
        preferred_element_type=jnp.float32,
    )
    put(grad_ref, unit * CG, grad)


def flat_quads(grad_ref, rows_count):
    for quad in range(CG // 4):
        parts = [None] * TAPS
        for j in range(4):
            line = rolled(strided(grad_ref, quad * 4 + j, rows_count, CG), 32 * j)
            for m in range(3):
                piece = line[:, m * 128:(m + 1) * 128]
                at = 2 * j + m
                parts[at] = piece if parts[at] is None else parts[at] + piece
        flat = jnp.concatenate(parts, axis=1).astype(jnp.bfloat16)
        yield slice(quad * QUAD, (quad + 1) * QUAD), flat


def grads_kernel(owned, per_tile, routes_ref, x_ref, dy_ref, got_ref, wire_ref, taps_ref, grad_ref):
    samples, top_count, _ = routes_ref.shape
    groups = wire_ref.shape[1]
    together = min(ROWS // groups, per_tile)
    rows_count = together * groups
    per_sample = per_tile // together
    tile = lax.axis_index("grid")
    mine = lax.axis_index("batch")
    grad_ref[WIDE // 128 - 1] = jnp.zeros((rows_count * CG, 128), jnp.float32)
    masks = pixel_masks(CG)

    def work(sample, block, read):
        for unit in range(rows_count):
            place = block * together + unit // groups
            span = pl.ds(pl.multiple_of(place * PIX, PIX), PIX)
            x, dy = read(unit % groups, span)
            unit_grad(x, dy, unit, taps_ref, grad_ref, masks)
        slots = []
        for place in range(together):
            column = tile * per_tile + block * together + place
            slots.append(
                [lax.div(routes_ref[sample, rank, column], owned) for rank in range(top_count)]
            )
        for lanes, flat in flat_quads(grad_ref, rows_count):
            for place in range(together):
                for slot in slots[place]:
                    wire_ref[slot, :, lanes] = flat[place * groups:(place + 1) * groups]

    def own(block, carry):
        def read(group, span):
            row = pl.multiple_of((mine * groups + group) * CG, CG)
            return tuple(ref[0, pl.ds(row, CG), span] for ref in (x_ref, dy_ref))

        work(mine, block, read)
        return carry

    def other(number, carry):
        step = lax.div(number, per_sample)

        def read(group, span):
            rows = slice(group * CG, (group + 1) * CG)
            return tuple(got_ref[step, which, rows, span] for which in range(2))

        work(lax.rem(mine - step - 1 + samples, samples), lax.rem(number, per_sample), read)
        return carry

    lax.fori_loop(0, per_sample, own, 0)
    lax.fori_loop(0, (samples - 1) * per_sample, other, 0)


def tables_kernel(owned, per_tile, routes_ref, logits_ref, local_ref, gate_ref):
    samples, top_count, _ = routes_ref.shape
    first = lax.axis_index("grid") * owned

    def scan(tile, carry):
        locals_hit, logits_hit = [], []
        for sample in range(samples):
            for rank in range(top_count):
                for place in range(per_tile):
                    at = (sample, rank, tile * per_tile + place)
                    inside = routes_ref[at] - first
                    hit = (inside >= 0) & (inside < owned)
                    locals_hit.append(jnp.where(hit, inside, 0))
                    logits_hit.append(jnp.where(hit, logits_ref[at], 0.0))
        local_ref[tile] = tree_sum(locals_hit)
        gate = jax.nn.sigmoid(jnp.full(gate_ref.shape[1:], tree_sum(logits_hit), jnp.float32))
        gate_ref[tile] = gate / SIDE
        return carry

    lax.fori_loop(0, local_ref.shape[0], scan, 0)


def adjoint_unit(mixed_ref, spread_ref, unit, dy, masks):
    kernel = joined(mixed_ref, unit * CG, CG)[:, :ROW].astype(jnp.bfloat16)
    spread = lax.dot_general(
        kernel, dy, (((0,), (0,)), ((), ())), preferred_element_type=jnp.float32
    )
    put(spread_ref, unit * ROW, spread)
    total = jnp.zeros((CG, PIX), jnp.float32)
    for tap in range(TAPS):
        part = strided(spread_ref, unit * ROW + tap, CG, TAPS)
        total += moved(part, 1 - tap // 3, 1 - tap % 3, masks)
    return total.astype(jnp.bfloat16)


def adjoint_kernel(owned, routes_ref, logits_ref, wire_ref, got_ref, *rest):
    pair_refs, rest = rest[:-12], rest[-12:]
    (
        out_ref, own_dots_ref, own_mixed_ref,
        grads_ref, dy_ref, kernels_ref, flat_ref, mixed_ref, spread_ref, dots_ref, place_sem,
        fetch_sem,
    ) = rest
    samples, top_count, patches = routes_ref.shape
    tiles, groups, _ = kernels_ref.shape
    channels = groups * CG
    per_tile = patches // tiles
    together = min(ROWS // groups, per_tile)
    rows_count = together * groups
    per_sample = per_tile // together
    tile = lax.axis_index("grid")
    mine = lax.axis_index("batch")
    places = [
        (source.at[which], kernels_ref.at[tile ^ (2 * pair + which)])
        for pair, source in zip(pair_order(tiles), pair_refs)
        for which in range(2)
    ]
    copies = [
        pltpu.make_async_copy(source, target, place_sem.at[number])
        for number, (source, target) in enumerate(places)
    ]
    copies.append(pltpu.make_async_copy(wire_ref, grads_ref, fetch_sem.at[0]))
    copies.append(pltpu.make_async_copy(got_ref.at[:, 1], dy_ref, fetch_sem.at[1]))
    for copy in copies:
        copy.start()
    masks = pixel_masks(CG)
    for copy in copies:
        copy.wait()

    def mix(block, target_ref):
        for place in range(together):
            patch = block * together + place
            sample = lax.div(patch, per_tile)
            column = tile * per_tile + lax.rem(patch, per_tile)
            gates, slots = [], []
            for rank in range(top_count):
                logit = logits_ref[sample, rank, column]
                gates.append(jax.nn.sigmoid(jnp.full((groups, 128), logit, jnp.float32)))
                slots.append(lax.div(routes_ref[sample, rank, column], owned))
            dots = [jnp.zeros((groups, 128), jnp.float32) for _ in range(top_count)]
            for at in range(0, CG * ROW, 128):
                lanes = slice(at, at + 128)
                mixed = jnp.zeros((groups, 128), jnp.float32)
                grad = grads_ref[slots[0], :, lanes].astype(jnp.float32)
                for rank in range(top_count):
                    kernel = kernels_ref[slots[rank], :, lanes].astype(jnp.float32)
                    dots[rank] += kernel * grad
                    mixed += gates[rank] * kernel
                flat_ref[place * groups:(place + 1) * groups, lanes] = mixed
            for rank in range(top_count):
                start = (block * top_count + rank) * rows_count + place * groups
                dots_ref[pl.ds(start, groups), :] = dots[rank]
        for quad in range(CG // 4):
            for j in range(4):
                start = quad * QUAD + 2 * j * 128
                line = rolled(flat_ref[:, start:start + WIDE], -32 * j)
                for m in range(WIDE // 128):
                    target_ref[m, pl.ds(quad * 4 + j, rows_count, stride=CG), :] = line[
                        :, m * 128:(m + 1) * 128
                    ]

    def work(number, carry):
        step = 1 + lax.div(number, per_sample)
        within = lax.rem(number, per_sample)
        block = lax.rem(mine + step, samples) * per_sample + within
        mix(block, mixed_ref)
        for unit in range(rows_count):
            place = unit // groups
            rows = slice((unit % groups) * CG, (unit % groups + 1) * CG)
            span = pl.ds(pl.multiple_of((within * together + place) * PIX, PIX), PIX)
            dy = dy_ref[samples - 1 - step, rows, span]
            out_ref[step - 1, rows, span] = adjoint_unit(
                mixed_ref, spread_ref, unit, dy, masks
            )
        return carry

    def own(within, carry):
        mix(mine * per_sample + within, own_mixed_ref.at[within])
        return carry

    lax.fori_loop(0, (samples - 1) * per_sample, work, 0)
    lax.fori_loop(0, per_sample, own, 0)
    count = samples * per_sample * top_count * rows_count
    sums = lax.dot_general(
        jnp.ones((DOT_ROWS, 128), jnp.float32),
        dots_ref[...],
        (((1,), (1,)), ((), ())),
        precision=lax.Precision.HIGHEST,
        preferred_element_type=jnp.float32,
    )
    row = lax.broadcasted_iota(jnp.int32, (count, 128), 0)
    lane = lax.broadcasted_iota(jnp.int32, (count, 128), 1)
    row_patch = row // (top_count * rows_count) * together + row % rows_count // groups
    row_rank = row // rows_count % top_count
    chosen = (lane == row_patch * top_count + row_rank).astype(jnp.float32)
    route_dots = lax.dot_general(
        sums,
        chosen,
        (((1,), (0,)), ((), ())),
        precision=lax.Precision.HIGHEST,
        preferred_element_type=jnp.float32,
    ).astype(jnp.bfloat16)
    own_dots_ref[...] = route_dots
    for step in range(1, samples):
        out_ref[step - 1, channels:channels + DOT_ROWS, :128] = route_dots


def own_adjoint_kernel(mixed_ref, dy_ref, out_ref, spread_ref):
    per_sample, _, mixed_rows, _ = mixed_ref.shape
    rows_count = mixed_rows // CG
    groups = out_ref.shape[0] // CG
    together = rows_count // groups
    mine = lax.axis_index("batch")
    masks = pixel_masks(CG)

    def work(within, carry):
        for unit in range(rows_count):
            place = within * together + unit // groups
            group = unit % groups
            lanes = pl.ds(pl.multiple_of(place * PIX, PIX), PIX)
            row = pl.multiple_of((mine * groups + group) * CG, CG)
            out_ref[group * CG:(group + 1) * CG, lanes] = adjoint_unit(
                mixed_ref.at[within], spread_ref, unit, dy_ref[0, pl.ds(row, CG), lanes], masks
            )
        return carry

    lax.fori_loop(0, per_sample, work, 0)


def sum_kernel(local_ref, gate_ref, got_ref, out_hbm, total_ref, sem):
    tiles, groups, width = got_ref.shape
    chunk = width // SUM_CHUNKS
    copies = []
    for part in range(SUM_CHUNKS):
        span = slice(part * chunk, (part + 1) * chunk)
        total_ref[:, :, span] = jnp.zeros(total_ref.shape[:2] + (chunk,), jnp.float32)

        def add(quad, carry):
            for tile in (quad * 4 + i for i in range(4)):
                local = local_ref[tile]
                gate = gate_ref[tile]
                for at in range(part * chunk, (part + 1) * chunk, 128):
                    lanes = slice(at, at + 128)
                    total_ref[local, :, lanes] += gate * got_ref[tile, :, lanes].astype(jnp.float32)
            return carry

        lax.fori_loop(0, tiles // 4, add, 0)
        copies.append(
            pltpu.make_async_copy(total_ref.at[:, :, span], out_hbm.at[:, :, span], sem.at[part])
        )
        copies[-1].start()
    for copy in copies:
        copy.wait()


def per_device(inputs, cotangent, weights, gate_logits, routes):
    tiles = lax.axis_size("grid")
    batch = lax.axis_size("batch")
    owned, groups, width = weights.shape
    samples, patches, top_count = routes.shape
    per_tile = patches // tiles
    span = inputs.shape[2]
    channels = groups * CG
    assert samples * per_tile * top_count == tiles and samples == batch
    smem = pl.BlockSpec(memory_space=pltpu.SMEM)
    vmem = pl.BlockSpec(memory_space=pltpu.VMEM)
    hbm = pl.BlockSpec(memory_space=pltpu.HBM)
    anywhere = pl.BlockSpec(memory_space=pl.ANY)
    params = pltpu.CompilerParams(vmem_limit_bytes=VMEM_LIMIT)
    routes_t = routes.transpose(0, 2, 1)
    logits_t = gate_logits.transpose(0, 2, 1)
    assert tiles & (tiles - 1) == 0 and tiles >= 4
    together = min(ROWS // groups, per_tile)
    rows = together * groups

    def blocks_shape(count):
        return jax.ShapeDtypeStruct((count, groups, width), jnp.bfloat16)

    def swap(blocks, step):
        return lax.ppermute(blocks, "grid", [(i, i ^ step) for i in range(tiles)])

    weights_beside = swap(weights, 1)
    pair_count = tiles // 2
    pairs = []
    order = pair_order(tiles)
    for some in (order[:EARLY], order[EARLY:]):
        pairs += pl.pallas_call(
            functools.partial(pack_kernel, owned, per_tile, some),
            out_shape=(blocks_shape(2),) * len(some),
            in_specs=[smem, vmem, vmem],
            out_specs=(hbm,) * len(some),
            scratch_shapes=[pltpu.SemaphoreType.DMA((pair_count, 2))],
            compiler_params=params,
            name="pack",
        )(routes_t, weights, weights_beside)
    pairs = [
        blocks if pair == 0 else swap(blocks, 2 * pair)
        for pair, blocks in zip(pair_order(tiles), pairs)
    ]

    def exchange(blocks):
        return [
            lax.ppermute(
                blocks[step - 1], "batch", [(i, (i + step) % batch) for i in range(batch)]
            )
            for step in range(1, batch)
        ]

    mine = lax.axis_index("batch")
    to_send = pl.pallas_call(
        stage_kernel,
        out_shape=jax.ShapeDtypeStruct((batch - 1, 2, channels, span), jnp.bfloat16),
        in_specs=[hbm] * 2,
        out_specs=hbm,
        scratch_shapes=[
            pltpu.VMEM((batch - 1, 2, channels, span), jnp.bfloat16),
            pltpu.SemaphoreType.DMA((batch - 1, 2)),
            pltpu.SemaphoreType.DMA((batch - 1, 2)),
        ],
        compiler_params=pltpu.CompilerParams(vmem_limit_bytes=WHOLE_VMEM),
        cost_estimate=pl.CostEstimate(flops=COST, bytes_accessed=1, transcendentals=0),
        name="stage",
    )(inputs, cotangent)
    got = jnp.stack(exchange([to_send[step] for step in range(batch - 1)]))

    grad_scratch = [
        pltpu.VMEM((PIX // 128, rows * ROW, 128), jnp.float32),
        pltpu.VMEM((WIDE // 128, rows * CG, 128), jnp.float32),
    ]
    wire = pl.pallas_call(
        functools.partial(grads_kernel, owned, per_tile),
        out_shape=blocks_shape(tiles),
        in_specs=[smem, vmem, vmem, vmem],
        out_specs=vmem,
        scratch_shapes=grad_scratch,
        compiler_params=params,
        cost_estimate=pl.CostEstimate(flops=COST, bytes_accessed=1, transcendentals=0),
        name="kernel_grads",
    )(routes_t, inputs, cotangent, got)

    wire, _ = lax.optimization_barrier((wire, pairs[:2]))
    grads_back = lax.all_to_all(wire, "grid", split_axis=0, concat_axis=0, tiled=True)

    per_sample = per_tile // together
    parts, own_dots, own_mixed = pl.pallas_call(
        functools.partial(adjoint_kernel, owned),
        out_shape=(
            jax.ShapeDtypeStruct((batch - 1, channels + DOT_ROWS, span), jnp.bfloat16),
            jax.ShapeDtypeStruct((DOT_ROWS, 128), jnp.bfloat16),
            jax.ShapeDtypeStruct((per_sample, WIDE // 128, rows * CG, 128), jnp.float32),
        ),
        in_specs=[smem, smem] + [anywhere] * (2 + pair_count),
        out_specs=(vmem, vmem, vmem),
        scratch_shapes=[
            pltpu.VMEM((tiles, groups, width), jnp.bfloat16),
            pltpu.VMEM((batch - 1, channels, span), jnp.bfloat16),
            pltpu.VMEM((tiles, groups, width), jnp.bfloat16),
            pltpu.VMEM((rows, width), jnp.float32),
            pltpu.VMEM((WIDE // 128, rows * CG, 128), jnp.float32),
            pltpu.VMEM((PIX // 128, rows * ROW, 128), jnp.float32),
            pltpu.VMEM((samples * per_tile * top_count * groups, 128), jnp.float32),
            pltpu.SemaphoreType.DMA((tiles,)),
            pltpu.SemaphoreType.DMA((2,)),
        ],
        compiler_params=params,
        cost_estimate=pl.CostEstimate(flops=COST, bytes_accessed=1, transcendentals=0),
        name="adjoint",
    )(routes_t, logits_t, wire, got, *pairs)

    own_part = pl.pallas_call(
        own_adjoint_kernel,
        out_shape=jax.ShapeDtypeStruct((channels, span), jnp.bfloat16),
        in_specs=[vmem, vmem],
        out_specs=vmem,
        scratch_shapes=[pltpu.VMEM((PIX // 128, rows * ROW, 128), jnp.float32)],
        compiler_params=params,
        cost_estimate=pl.CostEstimate(flops=COST // 20, bytes_accessed=1, transcendentals=0),
        name="own_adjoint",
    )(own_mixed, cotangent)

    late_routes, late_logits, _ = lax.optimization_barrier((routes_t, logits_t, own_dots))
    local, gate_table = pl.pallas_call(
        functools.partial(tables_kernel, owned, per_tile),
        out_shape=(
            jax.ShapeDtypeStruct((tiles,), jnp.int32),
            jax.ShapeDtypeStruct((tiles, groups, 128), jnp.float32),
        ),
        in_specs=[smem, smem],
        out_specs=(smem, vmem),
        compiler_params=params,
        name="tables",
    )(late_routes, late_logits)

    arrived = exchange([parts[step] for step in range(batch - 1)])
    d_inputs = jnp.zeros(inputs.shape, jnp.bfloat16)
    dots = own_dots[0].astype(jnp.float32)
    for step, part in enumerate([own_part] + arrived):
        block = lax.rem(mine - step + batch, batch)
        d_inputs = lax.dynamic_update_slice(
            d_inputs, part[None, :channels], (0, block * channels, 0)
        )
        if step:
            dots += part[channels, :128].astype(jnp.float32)
    dots = dots[:tiles].reshape(samples, per_tile, top_count)
    gates = jax.nn.sigmoid(
        lax.dynamic_slice_in_dim(late_logits, lax.axis_index("grid") * per_tile, per_tile, 2)
    ).transpose(0, 2, 1)
    gate_grad = gates * (1.0 - gates) * dots / SIDE

    d_weights = pl.pallas_call(
        sum_kernel,
        out_shape=jax.ShapeDtypeStruct(weights.shape, jnp.float32),
        in_specs=[smem, vmem, vmem],
        out_specs=hbm,
        scratch_shapes=[
            pltpu.VMEM(weights.shape, jnp.float32),
            pltpu.SemaphoreType.DMA((SUM_CHUNKS,)),
        ],
        compiler_params=params,
        name="weight_sum",
    )(local, gate_table, grads_back)
    return (d_inputs, d_weights, gate_grad)


def solution(mesh):
    placed = (
        P("batch", None, "grid"),
        P("batch", None, "grid"),
        P("grid", "batch", None),
        P(),
        P(),
    )
    return jax.shard_map(
        per_device,
        mesh=mesh,
        in_specs=placed,
        out_specs=(P("batch", None, "grid"), P("grid", "batch", None), P(None, "grid", None)),
        check_vma=False,
    )
```

```python
import functools

import jax
import jax.numpy as jnp
from jax import lax
from jax.experimental import pallas as pl
from jax.experimental.pallas import tpu as pltpu
from jax.sharding import PartitionSpec as P

CG = 32
SIDE = 16
PIX = SIDE * SIDE
TAPS = 9
ROW = CG * TAPS
WIDE = 384
QUAD = 4 * ROW
ROWS = 8
DOT_ROWS = 16
VMEM_LIMIT = 40 * 1024 * 1024
WHOLE_VMEM = 60 * 1024 * 1024
EARLY = 3
SUM_CHUNKS = 3
COST = 20_000_000_000


def rolled(values, shift):
    extent = values.shape[1]
    shift %= extent
    return values if shift == 0 else pltpu.roll(values, shift, 1)


def pixel_masks(rows):
    pixel = lax.broadcasted_iota(jnp.int32, (rows, PIX), 1)
    column = pixel % SIDE
    in_row = {-1: pixel >= SIDE, 0: None, 1: pixel < PIX - SIDE}
    in_column = {-1: column > 0, 0: None, 1: column < SIDE - 1}
    masks = {}
    for row_shift, row_mask in in_row.items():
        for column_shift, column_mask in in_column.items():
            both = [mask for mask in (row_mask, column_mask) if mask is not None]
            masks[row_shift, column_shift] = both[0] & both[-1] if both else None
    return masks


def moved(values, row_shift, column_shift, masks):
    out = rolled(values, -(row_shift * SIDE + column_shift))
    mask = masks[row_shift, column_shift]
    return out if mask is None else jnp.where(mask, out, 0.0)


def joined(ref, start, count):
    return jnp.concatenate([ref[m, start:start + count, :] for m in range(ref.shape[0])], axis=1)


def strided(ref, start, count, stride):
    return jnp.concatenate(
        [ref[m, pl.ds(start, count, stride=stride), :] for m in range(ref.shape[0])], axis=1
    )


def put(ref, start, values):
    for at in range(0, values.shape[1], 128):
        piece = values[:, at:at + 128]
        ref[at // 128, start:start + values.shape[0], :piece.shape[1]] = piece


def pair_order(tiles):
    near, far = list(range(tiles // 4)), list(range(tiles // 4, tiles // 2))
    first = far.pop(len(far) // 2)
    return [first] + near[1:2] + near[2:] + far + near[:1]


def tree_sum(values):
    while len(values) > 1:
        values = [sum(values[at:at + 2]) for at in range(0, len(values), 2)]
    return values[0]


def stage_kernel(x_hbm, dy_hbm, send_ref, halves_ref, halves_sem, send_sem):
    others, _, channels, _ = send_ref.shape
    mine = lax.axis_index("batch")
    taken, sent = [], []
    for step in range(1, others + 1):
        block = lax.rem(mine + step, others + 1)
        rows = pl.ds(pl.multiple_of(block * channels, channels), channels)
        for which, source in enumerate((x_hbm, dy_hbm)):
            at = (step - 1, which)
            taken.append(
                pltpu.make_async_copy(source.at[0, rows], halves_ref.at[at], halves_sem.at[at])
            )
            sent.append(
                pltpu.make_async_copy(halves_ref.at[at], send_ref.at[at], send_sem.at[at])
            )
    for copy in taken:
        copy.start()
    for copy, then in zip(taken, sent):
        copy.wait()
        then.start()
    for copy in sent:
        copy.wait()


def pack_kernel(owned, per_tile, pairs, routes_ref, own_ref, beside_ref, *rest):
    pair_refs, sem = rest[:-1], rest[-1]
    samples, top_count, _ = routes_ref.shape
    here = lax.axis_index("grid")
    copies = []
    for pair, target in zip(pairs, pair_refs):
        column = (here ^ (2 * pair)) * per_tile
        experts = [
            routes_ref[sample, rank, column + place]
            for sample in range(samples)
            for rank in range(top_count)
            for place in range(per_tile)
        ]
        for which, source in enumerate((own_ref, beside_ref)):
            inside = [expert - (here ^ which) * owned for expert in experts]
            found = tree_sum([jnp.where((at >= 0) & (at < owned), at, 0) for at in inside])
            copies.append(
                pltpu.make_async_copy(source.at[found], target.at[which], sem.at[pair, which])
            )
            copies[-1].start()
    for copy in copies:
        copy.wait()


def unit_grad(x, dy, unit, taps_ref, grad_ref, masks):
    x = x.astype(jnp.float32)
    for tap in range(TAPS):
        part = moved(x, tap // 3 - 1, tap % 3 - 1, masks)
        for half in range(PIX // 128):
            taps_ref[half, pl.ds(unit * ROW + tap, CG, stride=TAPS), :] = part[
                :, half * 128:(half + 1) * 128
            ]
    grad = lax.dot_general(
        dy,
        joined(taps_ref, unit * ROW, ROW).astype(jnp.bfloat16),
        (((1,), (1,)), ((), ())),
        preferred_element_type=jnp.float32,
    )
    put(grad_ref, unit * CG, grad)


def flat_quads(grad_ref, rows_count):
    for quad in range(CG // 4):
        parts = [None] * TAPS
        for j in range(4):
            line = rolled(strided(grad_ref, quad * 4 + j, rows_count, CG), 32 * j)
            for m in range(3):
                piece = line[:, m * 128:(m + 1) * 128]
                at = 2 * j + m
                parts[at] = piece if parts[at] is None else parts[at] + piece
        flat = jnp.concatenate(parts, axis=1).astype(jnp.bfloat16)
        yield slice(quad * QUAD, (quad + 1) * QUAD), flat


def grads_kernel(owned, per_tile, routes_ref, x_ref, dy_ref, got_ref, wire_ref, taps_ref, grad_ref):
    samples, top_count, _ = routes_ref.shape
    groups = wire_ref.shape[1]
    together = min(ROWS // groups, per_tile)
    rows_count = together * groups
    per_sample = per_tile // together
    tile = lax.axis_index("grid")
    mine = lax.axis_index("batch")
    grad_ref[WIDE // 128 - 1] = jnp.zeros((rows_count * CG, 128), jnp.float32)
    masks = pixel_masks(CG)

    def work(sample, block, read):
        for unit in range(rows_count):
            place = block * together + unit // groups
            span = pl.ds(pl.multiple_of(place * PIX, PIX), PIX)
            x, dy = read(unit % groups, span)
            unit_grad(x, dy, unit, taps_ref, grad_ref, masks)
        slots = []
        for place in range(together):
            column = tile * per_tile + block * together + place
            slots.append(
                [lax.div(routes_ref[sample, rank, column], owned) for rank in range(top_count)]
            )
        for lanes, flat in flat_quads(grad_ref, rows_count):
            for place in range(together):
                for slot in slots[place]:
                    wire_ref[slot, :, lanes] = flat[place * groups:(place + 1) * groups]

    def own(block, carry):
        def read(group, span):
            row = pl.multiple_of((mine * groups + group) * CG, CG)
            return tuple(ref[0, pl.ds(row, CG), span] for ref in (x_ref, dy_ref))

        work(mine, block, read)
        return carry

    def other(number, carry):
        step = lax.div(number, per_sample)

        def read(group, span):
            rows = slice(group * CG, (group + 1) * CG)
            return tuple(got_ref[step, which, rows, span] for which in range(2))

        work(lax.rem(mine - step - 1 + samples, samples), lax.rem(number, per_sample), read)
        return carry

    lax.fori_loop(0, per_sample, own, 0)
    lax.fori_loop(0, (samples - 1) * per_sample, other, 0)


def tables_kernel(owned, per_tile, routes_ref, logits_ref, local_ref, gate_ref):
    samples, top_count, _ = routes_ref.shape
    first = lax.axis_index("grid") * owned

    def scan(tile, carry):
        locals_hit, logits_hit = [], []
        for sample in range(samples):
            for rank in range(top_count):
                for place in range(per_tile):
                    at = (sample, rank, tile * per_tile + place)
                    inside = routes_ref[at] - first
                    hit = (inside >= 0) & (inside < owned)
                    locals_hit.append(jnp.where(hit, inside, 0))
                    logits_hit.append(jnp.where(hit, logits_ref[at], 0.0))
        local_ref[tile] = tree_sum(locals_hit)
        gate = jax.nn.sigmoid(jnp.full(gate_ref.shape[1:], tree_sum(logits_hit), jnp.float32))
        gate_ref[tile] = gate / SIDE
        return carry

    lax.fori_loop(0, local_ref.shape[0], scan, 0)


def adjoint_unit(mixed_ref, spread_ref, unit, dy, masks):
    kernel = joined(mixed_ref, unit * CG, CG)[:, :ROW].astype(jnp.bfloat16)
    spread = lax.dot_general(
        kernel, dy, (((0,), (0,)), ((), ())), preferred_element_type=jnp.float32
    )
    put(spread_ref, unit * ROW, spread)
    total = jnp.zeros((CG, PIX), jnp.float32)
    for tap in range(TAPS):
        part = strided(spread_ref, unit * ROW + tap, CG, TAPS)
        total += moved(part, 1 - tap // 3, 1 - tap % 3, masks)
    return total.astype(jnp.bfloat16)


def adjoint_kernel(owned, routes_ref, logits_ref, wire_ref, got_ref, *rest):
    pair_refs, rest = rest[:-12], rest[-12:]
    (
        out_ref, own_dots_ref, own_mixed_ref,
        grads_ref, dy_ref, kernels_ref, flat_ref, mixed_ref, spread_ref, dots_ref, place_sem,
        fetch_sem,
    ) = rest
    samples, top_count, patches = routes_ref.shape
    tiles, groups, _ = kernels_ref.shape
    channels = groups * CG
    per_tile = patches // tiles
    together = min(ROWS // groups, per_tile)
    rows_count = together * groups
    per_sample = per_tile // together
    tile = lax.axis_index("grid")
    mine = lax.axis_index("batch")
    places = [
        (source.at[which], kernels_ref.at[tile ^ (2 * pair + which)])
        for pair, source in zip(pair_order(tiles), pair_refs)
        for which in range(2)
    ]
    copies = [
        pltpu.make_async_copy(source, target, place_sem.at[number])
        for number, (source, target) in enumerate(places)
    ]
    copies.append(pltpu.make_async_copy(wire_ref, grads_ref, fetch_sem.at[0]))
    copies.append(pltpu.make_async_copy(got_ref.at[:, 1], dy_ref, fetch_sem.at[1]))
    for copy in copies:
        copy.start()
    masks = pixel_masks(CG)
    for copy in copies:
        copy.wait()

    def mix(block, target_ref):
        for place in range(together):
            patch = block * together + place
            sample = lax.div(patch, per_tile)
            column = tile * per_tile + lax.rem(patch, per_tile)
            gates, slots = [], []
            for rank in range(top_count):
                logit = logits_ref[sample, rank, column]
                gates.append(jax.nn.sigmoid(jnp.full((groups, 128), logit, jnp.float32)))
                slots.append(lax.div(routes_ref[sample, rank, column], owned))
            dots = [jnp.zeros((groups, 128), jnp.float32) for _ in range(top_count)]
            for at in range(0, CG * ROW, 128):
                lanes = slice(at, at + 128)
                mixed = jnp.zeros((groups, 128), jnp.float32)
                grad = grads_ref[slots[0], :, lanes].astype(jnp.float32)
                for rank in range(top_count):
                    kernel = kernels_ref[slots[rank], :, lanes].astype(jnp.float32)
                    dots[rank] += kernel * grad
                    mixed += gates[rank] * kernel
                flat_ref[place * groups:(place + 1) * groups, lanes] = mixed
            for rank in range(top_count):
                start = (block * top_count + rank) * rows_count + place * groups
                dots_ref[pl.ds(start, groups), :] = dots[rank]
        for quad in range(CG // 4):
            for j in range(4):
                start = quad * QUAD + 2 * j * 128
                line = rolled(flat_ref[:, start:start + WIDE], -32 * j)
                for m in range(WIDE // 128):
                    target_ref[m, pl.ds(quad * 4 + j, rows_count, stride=CG), :] = line[
                        :, m * 128:(m + 1) * 128
                    ]

    def work(number, carry):
        step = 1 + lax.div(number, per_sample)
        within = lax.rem(number, per_sample)
        block = lax.rem(mine + step, samples) * per_sample + within
        mix(block, mixed_ref)
        for unit in range(rows_count):
            place = unit // groups
            rows = slice((unit % groups) * CG, (unit % groups + 1) * CG)
            span = pl.ds(pl.multiple_of((within * together + place) * PIX, PIX), PIX)
            dy = dy_ref[samples - 1 - step, rows, span]
            out_ref[step - 1, rows, span] = adjoint_unit(
                mixed_ref, spread_ref, unit, dy, masks
            )
        return carry

    def own(within, carry):
        mix(mine * per_sample + within, own_mixed_ref.at[within])
        return carry

    lax.fori_loop(0, (samples - 1) * per_sample, work, 0)
    lax.fori_loop(0, per_sample, own, 0)
    count = samples * per_sample * top_count * rows_count
    sums = lax.dot_general(
        jnp.ones((DOT_ROWS, 128), jnp.float32),
        dots_ref[...],
        (((1,), (1,)), ((), ())),
        precision=lax.Precision.HIGHEST,
        preferred_element_type=jnp.float32,
    )
    row = lax.broadcasted_iota(jnp.int32, (count, 128), 0)
    lane = lax.broadcasted_iota(jnp.int32, (count, 128), 1)
    row_patch = row // (top_count * rows_count) * together + row % rows_count // groups
    row_rank = row // rows_count % top_count
    chosen = (lane == row_patch * top_count + row_rank).astype(jnp.float32)
    route_dots = lax.dot_general(
        sums,
        chosen,
        (((1,), (0,)), ((), ())),
        precision=lax.Precision.HIGHEST,
        preferred_element_type=jnp.float32,
    ).astype(jnp.bfloat16)
    own_dots_ref[...] = route_dots
    for step in range(1, samples):
        out_ref[step - 1, channels:channels + DOT_ROWS, :128] = route_dots


def own_adjoint_kernel(mixed_ref, dy_ref, out_ref, spread_ref):
    per_sample, _, mixed_rows, _ = mixed_ref.shape
    rows_count = mixed_rows // CG
    groups = out_ref.shape[0] // CG
    together = rows_count // groups
    mine = lax.axis_index("batch")
    masks = pixel_masks(CG)

    def work(within, carry):
        for unit in range(rows_count):
            place = within * together + unit // groups
            group = unit % groups
            lanes = pl.ds(pl.multiple_of(place * PIX, PIX), PIX)
            row = pl.multiple_of((mine * groups + group) * CG, CG)
            out_ref[group * CG:(group + 1) * CG, lanes] = adjoint_unit(
                mixed_ref.at[within], spread_ref, unit, dy_ref[0, pl.ds(row, CG), lanes], masks
            )
        return carry

    lax.fori_loop(0, per_sample, work, 0)


def sum_kernel(local_ref, gate_ref, got_ref, out_hbm, total_ref, sem):
    tiles, groups, width = got_ref.shape
    chunk = width // SUM_CHUNKS
    copies = []
    for part in range(SUM_CHUNKS):
        span = slice(part * chunk, (part + 1) * chunk)
        total_ref[:, :, span] = jnp.zeros(total_ref.shape[:2] + (chunk,), jnp.float32)

        def add(quad, carry):
            for tile in (quad * 4 + i for i in range(4)):
                local = local_ref[tile]
                gate = gate_ref[tile]
                for at in range(part * chunk, (part + 1) * chunk, 128):
                    lanes = slice(at, at + 128)
                    total_ref[local, :, lanes] += gate * got_ref[tile, :, lanes].astype(jnp.float32)
            return carry

        lax.fori_loop(0, tiles // 4, add, 0)
        copies.append(
            pltpu.make_async_copy(total_ref.at[:, :, span], out_hbm.at[:, :, span], sem.at[part])
        )
        copies[-1].start()
    for copy in copies:
        copy.wait()


def per_device(inputs, cotangent, weights, gate_logits, routes):
    tiles = lax.axis_size("grid")
    batch = lax.axis_size("batch")
    owned, groups, width = weights.shape
    samples, patches, top_count = routes.shape
    per_tile = patches // tiles
    span = inputs.shape[2]
    channels = groups * CG
    assert samples * per_tile * top_count == tiles and samples == batch
    smem = pl.BlockSpec(memory_space=pltpu.SMEM)
    vmem = pl.BlockSpec(memory_space=pltpu.VMEM)
    hbm = pl.BlockSpec(memory_space=pltpu.HBM)
    anywhere = pl.BlockSpec(memory_space=pl.ANY)
    params = pltpu.CompilerParams(vmem_limit_bytes=VMEM_LIMIT)
    routes_t = routes.transpose(0, 2, 1)
    logits_t = gate_logits.transpose(0, 2, 1)
    assert tiles & (tiles - 1) == 0 and tiles >= 4
    together = min(ROWS // groups, per_tile)
    rows = together * groups

    def blocks_shape(count):
        return jax.ShapeDtypeStruct((count, groups, width), jnp.bfloat16)

    def swap(blocks, step):
        return lax.ppermute(blocks, "grid", [(i, i ^ step) for i in range(tiles)])

    weights_beside = swap(weights, 1)
    pair_count = tiles // 2
    pairs = []
    order = pair_order(tiles)
    for some in (order[:EARLY], order[EARLY:]):
        pairs += pl.pallas_call(
            functools.partial(pack_kernel, owned, per_tile, some),
            out_shape=(blocks_shape(2),) * len(some),
            in_specs=[smem, vmem, vmem],
            out_specs=(hbm,) * len(some),
            scratch_shapes=[pltpu.SemaphoreType.DMA((pair_count, 2))],
            compiler_params=params,
            name="pack",
        )(routes_t, weights, weights_beside)
    pairs = [
        blocks if pair == 0 else swap(blocks, 2 * pair)
        for pair, blocks in zip(pair_order(tiles), pairs)
    ]

    def exchange(blocks):
        return [
            lax.ppermute(
                blocks[step - 1], "batch", [(i, (i + step) % batch) for i in range(batch)]
            )
            for step in range(1, batch)
        ]

    mine = lax.axis_index("batch")
    to_send = pl.pallas_call(
        stage_kernel,
        out_shape=jax.ShapeDtypeStruct((batch - 1, 2, channels, span), jnp.bfloat16),
        in_specs=[hbm] * 2,
        out_specs=hbm,
        scratch_shapes=[
            pltpu.VMEM((batch - 1, 2, channels, span), jnp.bfloat16),
            pltpu.SemaphoreType.DMA((batch - 1, 2)),
            pltpu.SemaphoreType.DMA((batch - 1, 2)),
        ],
        compiler_params=pltpu.CompilerParams(vmem_limit_bytes=WHOLE_VMEM),
        cost_estimate=pl.CostEstimate(flops=COST, bytes_accessed=1, transcendentals=0),
        name="stage",
    )(inputs, cotangent)
    got = jnp.stack(exchange([to_send[step] for step in range(batch - 1)]))

    grad_scratch = [
        pltpu.VMEM((PIX // 128, rows * ROW, 128), jnp.float32),
        pltpu.VMEM((WIDE // 128, rows * CG, 128), jnp.float32),
    ]
    wire = pl.pallas_call(
        functools.partial(grads_kernel, owned, per_tile),
        out_shape=blocks_shape(tiles),
        in_specs=[smem, vmem, vmem, vmem],
        out_specs=vmem,
        scratch_shapes=grad_scratch,
        compiler_params=params,
        cost_estimate=pl.CostEstimate(flops=COST, bytes_accessed=1, transcendentals=0),
        name="kernel_grads",
    )(routes_t, inputs, cotangent, got)

    wire, _ = lax.optimization_barrier((wire, pairs[:2]))
    grads_back = lax.all_to_all(wire, "grid", split_axis=0, concat_axis=0, tiled=True)

    per_sample = per_tile // together
    parts, own_dots, own_mixed = pl.pallas_call(
        functools.partial(adjoint_kernel, owned),
        out_shape=(
            jax.ShapeDtypeStruct((batch - 1, channels + DOT_ROWS, span), jnp.bfloat16),
            jax.ShapeDtypeStruct((DOT_ROWS, 128), jnp.bfloat16),
            jax.ShapeDtypeStruct((per_sample, WIDE // 128, rows * CG, 128), jnp.float32),
        ),
        in_specs=[smem, smem] + [anywhere] * (2 + pair_count),
        out_specs=(vmem, vmem, vmem),
        scratch_shapes=[
            pltpu.VMEM((tiles, groups, width), jnp.bfloat16),
            pltpu.VMEM((batch - 1, channels, span), jnp.bfloat16),
            pltpu.VMEM((tiles, groups, width), jnp.bfloat16),
            pltpu.VMEM((rows, width), jnp.float32),
            pltpu.VMEM((WIDE // 128, rows * CG, 128), jnp.float32),
            pltpu.VMEM((PIX // 128, rows * ROW, 128), jnp.float32),
            pltpu.VMEM((samples * per_tile * top_count * groups, 128), jnp.float32),
            pltpu.SemaphoreType.DMA((tiles,)),
            pltpu.SemaphoreType.DMA((2,)),
        ],
        compiler_params=params,
        cost_estimate=pl.CostEstimate(flops=COST, bytes_accessed=1, transcendentals=0),
        name="adjoint",
    )(routes_t, logits_t, wire, got, *pairs)

    own_part = pl.pallas_call(
        own_adjoint_kernel,
        out_shape=jax.ShapeDtypeStruct((channels, span), jnp.bfloat16),
        in_specs=[vmem, vmem],
        out_specs=vmem,
        scratch_shapes=[pltpu.VMEM((PIX // 128, rows * ROW, 128), jnp.float32)],
        compiler_params=params,
        cost_estimate=pl.CostEstimate(flops=COST // 20, bytes_accessed=1, transcendentals=0),
        name="own_adjoint",
    )(own_mixed, cotangent)

    late_routes, late_logits, _ = lax.optimization_barrier((routes_t, logits_t, own_dots))
    local, gate_table = pl.pallas_call(
        functools.partial(tables_kernel, owned, per_tile),
        out_shape=(
            jax.ShapeDtypeStruct((tiles,), jnp.int32),
            jax.ShapeDtypeStruct((tiles, groups, 128), jnp.float32),
        ),
        in_specs=[smem, smem],
        out_specs=(smem, vmem),
        compiler_params=params,
        name="tables",
    )(late_routes, late_logits)

    arrived = exchange([parts[step] for step in range(batch - 1)])
    d_inputs = jnp.zeros(inputs.shape, jnp.bfloat16)
    dots = own_dots[0].astype(jnp.float32)
    for step, part in enumerate([own_part] + arrived):
        block = lax.rem(mine - step + batch, batch)
        d_inputs = lax.dynamic_update_slice(
            d_inputs, part[None, :channels], (0, block * channels, 0)
        )
        if step:
            dots += part[channels, :128].astype(jnp.float32)
    dots = dots[:tiles].reshape(samples, per_tile, top_count)
    gates = jax.nn.sigmoid(
        lax.dynamic_slice_in_dim(late_logits, lax.axis_index("grid") * per_tile, per_tile, 2)
    ).transpose(0, 2, 1)
    gate_grad = gates * (1.0 - gates) * dots / SIDE

    d_weights = pl.pallas_call(
        sum_kernel,
        out_shape=jax.ShapeDtypeStruct(weights.shape, jnp.float32),
        in_specs=[smem, vmem, vmem],
        out_specs=hbm,
        scratch_shapes=[
            pltpu.VMEM(weights.shape, jnp.float32),
            pltpu.SemaphoreType.DMA((SUM_CHUNKS,)),
        ],
        compiler_params=params,
        name="weight_sum",
    )(local, gate_table, grads_back)
    return (d_inputs, d_weights, gate_grad)


def solution(mesh):
    placed = (
        P("batch", None, "grid"),
        P("batch", None, "grid"),
        P("grid", "batch", None),
        P(),
        P(),
    )
    return jax.shard_map(
        per_device,
        mesh=mesh,
        in_specs=placed,
        out_specs=(P("batch", None, "grid"), P("grid", "batch", None), P(None, "grid", None)),
        check_vma=False,
    )
```

```python
import functools

import jax
import jax.numpy as jnp
from jax import lax
from jax.experimental import pallas as pl
from jax.experimental.pallas import tpu as pltpu
from jax.sharding import PartitionSpec as P

CG = 32
SIDE = 16
PIX = SIDE * SIDE
TAPS = 9
ROW = CG * TAPS
WIDE = 384
QUAD = 4 * ROW
ROWS = 8
DOT_ROWS = 16
VMEM_LIMIT = 40 * 1024 * 1024
WHOLE_VMEM = 60 * 1024 * 1024
EARLY = 3
SUM_CHUNKS = 3
COST = 20_000_000_000


def rolled(values, shift):
    extent = values.shape[1]
    shift %= extent
    return values if shift == 0 else pltpu.roll(values, shift, 1)


def pixel_masks(rows):
    pixel = lax.broadcasted_iota(jnp.int32, (rows, PIX), 1)
    column = pixel % SIDE
    in_row = {-1: pixel >= SIDE, 0: None, 1: pixel < PIX - SIDE}
    in_column = {-1: column > 0, 0: None, 1: column < SIDE - 1}
    masks = {}
    for row_shift, row_mask in in_row.items():
        for column_shift, column_mask in in_column.items():
            both = [mask for mask in (row_mask, column_mask) if mask is not None]
            masks[row_shift, column_shift] = both[0] & both[-1] if both else None
    return masks


def moved(values, row_shift, column_shift, masks):
    out = rolled(values, -(row_shift * SIDE + column_shift))
    mask = masks[row_shift, column_shift]
    return out if mask is None else jnp.where(mask, out, 0.0)


def joined(ref, start, count):
    return jnp.concatenate([ref[m, start:start + count, :] for m in range(ref.shape[0])], axis=1)


def strided(ref, start, count, stride):
    return jnp.concatenate(
        [ref[m, pl.ds(start, count, stride=stride), :] for m in range(ref.shape[0])], axis=1
    )


def put(ref, start, values):
    for at in range(0, values.shape[1], 128):
        piece = values[:, at:at + 128]
        ref[at // 128, start:start + values.shape[0], :piece.shape[1]] = piece


def pair_order(tiles):
    near, far = list(range(tiles // 4)), list(range(tiles // 4, tiles // 2))
    first = far.pop(len(far) // 2)
    return [first] + near[1:2] + near[2:] + far + near[:1]


def tree_sum(values):
    while len(values) > 1:
        values = [sum(values[at:at + 2]) for at in range(0, len(values), 2)]
    return values[0]


def stage_kernel(x_hbm, dy_hbm, send_ref, halves_ref, halves_sem, send_sem):
    others, _, channels, _ = send_ref.shape
    mine = lax.axis_index("batch")
    taken, sent = [], []
    for step in range(1, others + 1):
        block = lax.rem(mine + step, others + 1)
        rows = pl.ds(pl.multiple_of(block * channels, channels), channels)
        for which, source in enumerate((x_hbm, dy_hbm)):
            at = (step - 1, which)
            taken.append(
                pltpu.make_async_copy(source.at[0, rows], halves_ref.at[at], halves_sem.at[at])
            )
            sent.append(
                pltpu.make_async_copy(halves_ref.at[at], send_ref.at[at], send_sem.at[at])
            )
    for copy in taken:
        copy.start()
    for copy, then in zip(taken, sent):
        copy.wait()
        then.start()
    for copy in sent:
        copy.wait()


def pack_kernel(owned, per_tile, pairs, routes_ref, own_ref, beside_ref, *rest):
    pair_refs, sem = rest[:-1], rest[-1]
    samples, top_count, _ = routes_ref.shape
    here = lax.axis_index("grid")
    copies = []
    for pair, target in zip(pairs, pair_refs):
        column = (here ^ (2 * pair)) * per_tile
        experts = [
            routes_ref[sample, rank, column + place]
            for sample in range(samples)
            for rank in range(top_count)
            for place in range(per_tile)
        ]
        for which, source in enumerate((own_ref, beside_ref)):
            inside = [expert - (here ^ which) * owned for expert in experts]
            found = tree_sum([jnp.where((at >= 0) & (at < owned), at, 0) for at in inside])
            copies.append(
                pltpu.make_async_copy(source.at[found], target.at[which], sem.at[pair, which])
            )
            copies[-1].start()
    for copy in copies:
        copy.wait()


def unit_grad(x, dy, unit, taps_ref, grad_ref, masks):
    x = x.astype(jnp.float32)
    for tap in range(TAPS):
        part = moved(x, tap // 3 - 1, tap % 3 - 1, masks)
        for half in range(PIX // 128):
            taps_ref[half, pl.ds(unit * ROW + tap, CG, stride=TAPS), :] = part[
                :, half * 128:(half + 1) * 128
            ]
    grad = lax.dot_general(
        dy,
        joined(taps_ref, unit * ROW, ROW).astype(jnp.bfloat16),
        (((1,), (1,)), ((), ())),
        preferred_element_type=jnp.float32,
    )
    put(grad_ref, unit * CG, grad)


def flat_quads(grad_ref, rows_count):
    for quad in range(CG // 4):
        parts = [None] * TAPS
        for j in range(4):
            line = rolled(strided(grad_ref, quad * 4 + j, rows_count, CG), 32 * j)
            for m in range(3):
                piece = line[:, m * 128:(m + 1) * 128]
                at = 2 * j + m
                parts[at] = piece if parts[at] is None else parts[at] + piece
        flat = jnp.concatenate(parts, axis=1).astype(jnp.bfloat16)
        yield slice(quad * QUAD, (quad + 1) * QUAD), flat


def grads_kernel(owned, per_tile, routes_ref, x_ref, dy_ref, got_ref, wire_ref, taps_ref, grad_ref):
    samples, top_count, _ = routes_ref.shape
    groups = wire_ref.shape[1]
    together = min(ROWS // groups, per_tile)
    rows_count = together * groups
    per_sample = per_tile // together
    tile = lax.axis_index("grid")
    mine = lax.axis_index("batch")
    grad_ref[WIDE // 128 - 1] = jnp.zeros((rows_count * CG, 128), jnp.float32)
    masks = pixel_masks(CG)

    def work(sample, block, read):
        for unit in range(rows_count):
            place = block * together + unit // groups
            span = pl.ds(pl.multiple_of(place * PIX, PIX), PIX)
            x, dy = read(unit % groups, span)
            unit_grad(x, dy, unit, taps_ref, grad_ref, masks)
        slots = []
        for place in range(together):
            column = tile * per_tile + block * together + place
            slots.append(
                [lax.div(routes_ref[sample, rank, column], owned) for rank in range(top_count)]
            )
        for lanes, flat in flat_quads(grad_ref, rows_count):
            for place in range(together):
                for slot in slots[place]:
                    wire_ref[slot, :, lanes] = flat[place * groups:(place + 1) * groups]

    def own(block, carry):
        def read(group, span):
            row = pl.multiple_of((mine * groups + group) * CG, CG)
            return tuple(ref[0, pl.ds(row, CG), span] for ref in (x_ref, dy_ref))

        work(mine, block, read)
        return carry

    def other(number, carry):
        step = lax.div(number, per_sample)

        def read(group, span):
            rows = slice(group * CG, (group + 1) * CG)
            return tuple(got_ref[step, which, rows, span] for which in range(2))

        work(lax.rem(mine - step - 1 + samples, samples), lax.rem(number, per_sample), read)
        return carry

    lax.fori_loop(0, per_sample, own, 0)
    lax.fori_loop(0, (samples - 1) * per_sample, other, 0)


def tables_kernel(owned, per_tile, routes_ref, logits_ref, local_ref, gate_ref):
    samples, top_count, _ = routes_ref.shape
    first = lax.axis_index("grid") * owned

    def scan(tile, carry):
        locals_hit, logits_hit = [], []
        for sample in range(samples):
            for rank in range(top_count):
                for place in range(per_tile):
                    at = (sample, rank, tile * per_tile + place)
                    inside = routes_ref[at] - first
                    hit = (inside >= 0) & (inside < owned)
                    locals_hit.append(jnp.where(hit, inside, 0))
                    logits_hit.append(jnp.where(hit, logits_ref[at], 0.0))
        local_ref[tile] = tree_sum(locals_hit)
        gate = jax.nn.sigmoid(jnp.full(gate_ref.shape[1:], tree_sum(logits_hit), jnp.float32))
        gate_ref[tile] = gate / SIDE
        return carry

    lax.fori_loop(0, local_ref.shape[0], scan, 0)


def adjoint_unit(mixed_ref, spread_ref, unit, dy, masks):
    kernel = joined(mixed_ref, unit * CG, CG)[:, :ROW].astype(jnp.bfloat16)
    spread = lax.dot_general(
        kernel, dy, (((0,), (0,)), ((), ())), preferred_element_type=jnp.float32
    )
    put(spread_ref, unit * ROW, spread)
    total = jnp.zeros((CG, PIX), jnp.float32)
    for tap in range(TAPS):
        part = strided(spread_ref, unit * ROW + tap, CG, TAPS)
        total += moved(part, 1 - tap // 3, 1 - tap % 3, masks)
    return total.astype(jnp.bfloat16)


def adjoint_kernel(owned, routes_ref, logits_ref, wire_ref, got_ref, *rest):
    pair_refs, rest = rest[:-12], rest[-12:]
    (
        out_ref, own_dots_ref, own_mixed_ref,
        grads_ref, dy_ref, kernels_ref, flat_ref, mixed_ref, spread_ref, dots_ref, place_sem,
        fetch_sem,
    ) = rest
    samples, top_count, patches = routes_ref.shape
    tiles, groups, _ = kernels_ref.shape
    channels = groups * CG
    per_tile = patches // tiles
    together = min(ROWS // groups, per_tile)
    rows_count = together * groups
    per_sample = per_tile // together
    tile = lax.axis_index("grid")
    mine = lax.axis_index("batch")
    places = [
        (source.at[which], kernels_ref.at[tile ^ (2 * pair + which)])
        for pair, source in zip(pair_order(tiles), pair_refs)
        for which in range(2)
    ]
    copies = [
        pltpu.make_async_copy(source, target, place_sem.at[number])
        for number, (source, target) in enumerate(places)
    ]
    copies.append(pltpu.make_async_copy(wire_ref, grads_ref, fetch_sem.at[0]))
    copies.append(pltpu.make_async_copy(got_ref.at[:, 1], dy_ref, fetch_sem.at[1]))
    for copy in copies:
        copy.start()
    masks = pixel_masks(CG)
    for copy in copies:
        copy.wait()

    def mix(block, target_ref):
        for place in range(together):
            patch = block * together + place
            sample = lax.div(patch, per_tile)
            column = tile * per_tile + lax.rem(patch, per_tile)
            gates, slots = [], []
            for rank in range(top_count):
                logit = logits_ref[sample, rank, column]
                gates.append(jax.nn.sigmoid(jnp.full((groups, 128), logit, jnp.float32)))
                slots.append(lax.div(routes_ref[sample, rank, column], owned))
            dots = [jnp.zeros((groups, 128), jnp.float32) for _ in range(top_count)]
            for at in range(0, CG * ROW, 128):
                lanes = slice(at, at + 128)
                mixed = jnp.zeros((groups, 128), jnp.float32)
                grad = grads_ref[slots[0], :, lanes].astype(jnp.float32)
                for rank in range(top_count):
                    kernel = kernels_ref[slots[rank], :, lanes].astype(jnp.float32)
                    dots[rank] += kernel * grad
                    mixed += gates[rank] * kernel
                flat_ref[place * groups:(place + 1) * groups, lanes] = mixed
            for rank in range(top_count):
                start = (block * top_count + rank) * rows_count + place * groups
                dots_ref[pl.ds(start, groups), :] = dots[rank]
        for quad in range(CG // 4):
            for j in range(4):
                start = quad * QUAD + 2 * j * 128
                line = rolled(flat_ref[:, start:start + WIDE], -32 * j)
                for m in range(WIDE // 128):
                    target_ref[m, pl.ds(quad * 4 + j, rows_count, stride=CG), :] = line[
                        :, m * 128:(m + 1) * 128
                    ]

    def work(number, carry):
        step = 1 + lax.div(number, per_sample)
        within = lax.rem(number, per_sample)
        block = lax.rem(mine + step, samples) * per_sample + within
        mix(block, mixed_ref)
        for unit in range(rows_count):
            place = unit // groups
            rows = slice((unit % groups) * CG, (unit % groups + 1) * CG)
            span = pl.ds(pl.multiple_of((within * together + place) * PIX, PIX), PIX)
            dy = dy_ref[samples - 1 - step, rows, span]
            out_ref[step - 1, rows, span] = adjoint_unit(
                mixed_ref, spread_ref, unit, dy, masks
            )
        return carry

    def own(within, carry):
        mix(mine * per_sample + within, own_mixed_ref.at[within])
        return carry

    lax.fori_loop(0, (samples - 1) * per_sample, work, 0)
    lax.fori_loop(0, per_sample, own, 0)
    count = samples * per_sample * top_count * rows_count
    sums = lax.dot_general(
        jnp.ones((DOT_ROWS, 128), jnp.float32),
        dots_ref[...],
        (((1,), (1,)), ((), ())),
        precision=lax.Precision.HIGHEST,
        preferred_element_type=jnp.float32,
    )
    row = lax.broadcasted_iota(jnp.int32, (count, 128), 0)
    lane = lax.broadcasted_iota(jnp.int32, (count, 128), 1)
    row_patch = row // (top_count * rows_count) * together + row % rows_count // groups
    row_rank = row // rows_count % top_count
    chosen = (lane == row_patch * top_count + row_rank).astype(jnp.float32)
    route_dots = lax.dot_general(
        sums,
        chosen,
        (((1,), (0,)), ((), ())),
        precision=lax.Precision.HIGHEST,
        preferred_element_type=jnp.float32,
    ).astype(jnp.bfloat16)
    own_dots_ref[...] = route_dots
    for step in range(1, samples):
        out_ref[step - 1, channels:channels + DOT_ROWS, :128] = route_dots


def own_adjoint_kernel(mixed_ref, dy_ref, out_ref, spread_ref):
    per_sample, _, mixed_rows, _ = mixed_ref.shape
    rows_count = mixed_rows // CG
    groups = out_ref.shape[0] // CG
    together = rows_count // groups
    mine = lax.axis_index("batch")
    masks = pixel_masks(CG)

    def work(within, carry):
        for unit in range(rows_count):
            place = within * together + unit // groups
            group = unit % groups
            lanes = pl.ds(pl.multiple_of(place * PIX, PIX), PIX)
            row = pl.multiple_of((mine * groups + group) * CG, CG)
            out_ref[group * CG:(group + 1) * CG, lanes] = adjoint_unit(
                mixed_ref.at[within], spread_ref, unit, dy_ref[0, pl.ds(row, CG), lanes], masks
            )
        return carry

    lax.fori_loop(0, per_sample, work, 0)


def sum_kernel(local_ref, gate_ref, got_ref, out_hbm, total_ref, sem):
    tiles, groups, width = got_ref.shape
    chunk = width // SUM_CHUNKS
    unroll = min(tiles, 8)
    copies = []
    for part in range(SUM_CHUNKS):
        span = slice(part * chunk, (part + 1) * chunk)
        total_ref[:, :, span] = jnp.zeros(total_ref.shape[:2] + (chunk,), jnp.float32)

        def add(group, carry):
            for tile in (group * unroll + i for i in range(unroll)):
                local = local_ref[tile]
                gate = gate_ref[tile]
                for at in range(part * chunk, (part + 1) * chunk, 128):
                    lanes = slice(at, at + 128)
                    total_ref[local, :, lanes] += gate * got_ref[tile, :, lanes].astype(jnp.float32)
            return carry

        lax.fori_loop(0, tiles // unroll, add, 0)
        copies.append(
            pltpu.make_async_copy(total_ref.at[:, :, span], out_hbm.at[:, :, span], sem.at[part])
        )
        copies[-1].start()
    for copy in copies:
        copy.wait()


def per_device(inputs, cotangent, weights, gate_logits, routes):
    tiles = lax.axis_size("grid")
    batch = lax.axis_size("batch")
    owned, groups, width = weights.shape
    samples, patches, top_count = routes.shape
    per_tile = patches // tiles
    span = inputs.shape[2]
    channels = groups * CG
    assert samples * per_tile * top_count == tiles and samples == batch
    smem = pl.BlockSpec(memory_space=pltpu.SMEM)
    vmem = pl.BlockSpec(memory_space=pltpu.VMEM)
    hbm = pl.BlockSpec(memory_space=pltpu.HBM)
    anywhere = pl.BlockSpec(memory_space=pl.ANY)
    params = pltpu.CompilerParams(vmem_limit_bytes=VMEM_LIMIT)
    routes_t = routes.transpose(0, 2, 1)
    logits_t = gate_logits.transpose(0, 2, 1)
    assert tiles & (tiles - 1) == 0 and tiles >= 4
    together = min(ROWS // groups, per_tile)
    rows = together * groups

    def blocks_shape(count):
        return jax.ShapeDtypeStruct((count, groups, width), jnp.bfloat16)

    def swap(blocks, step):
        return lax.ppermute(blocks, "grid", [(i, i ^ step) for i in range(tiles)])

    weights_beside = swap(weights, 1)
    pair_count = tiles // 2
    pairs = []
    order = pair_order(tiles)
    for some in (order[:EARLY], order[EARLY:]):
        pairs += pl.pallas_call(
            functools.partial(pack_kernel, owned, per_tile, some),
            out_shape=(blocks_shape(2),) * len(some),
            in_specs=[smem, vmem, vmem],
            out_specs=(hbm,) * len(some),
            scratch_shapes=[pltpu.SemaphoreType.DMA((pair_count, 2))],
            compiler_params=params,
            name="pack",
        )(routes_t, weights, weights_beside)
    pairs = [
        blocks if pair == 0 else swap(blocks, 2 * pair)
        for pair, blocks in zip(pair_order(tiles), pairs)
    ]

    def exchange(blocks):
        return [
            lax.ppermute(
                blocks[step - 1], "batch", [(i, (i + step) % batch) for i in range(batch)]
            )
            for step in range(1, batch)
        ]

    mine = lax.axis_index("batch")
    to_send = pl.pallas_call(
        stage_kernel,
        out_shape=jax.ShapeDtypeStruct((batch - 1, 2, channels, span), jnp.bfloat16),
        in_specs=[hbm] * 2,
        out_specs=hbm,
        scratch_shapes=[
            pltpu.VMEM((batch - 1, 2, channels, span), jnp.bfloat16),
            pltpu.SemaphoreType.DMA((batch - 1, 2)),
            pltpu.SemaphoreType.DMA((batch - 1, 2)),
        ],
        compiler_params=pltpu.CompilerParams(vmem_limit_bytes=WHOLE_VMEM),
        cost_estimate=pl.CostEstimate(flops=COST, bytes_accessed=1, transcendentals=0),
        name="stage",
    )(inputs, cotangent)
    got = jnp.stack(exchange([to_send[step] for step in range(batch - 1)]))

    grad_scratch = [
        pltpu.VMEM((PIX // 128, rows * ROW, 128), jnp.float32),
        pltpu.VMEM((WIDE // 128, rows * CG, 128), jnp.float32),
    ]
    wire = pl.pallas_call(
        functools.partial(grads_kernel, owned, per_tile),
        out_shape=blocks_shape(tiles),
        in_specs=[smem, vmem, vmem, vmem],
        out_specs=vmem,
        scratch_shapes=grad_scratch,
        compiler_params=params,
        cost_estimate=pl.CostEstimate(flops=COST, bytes_accessed=1, transcendentals=0),
        name="kernel_grads",
    )(routes_t, inputs, cotangent, got)

    wire, _ = lax.optimization_barrier((wire, pairs[:2]))
    grads_back = lax.all_to_all(wire, "grid", split_axis=0, concat_axis=0, tiled=True)

    per_sample = per_tile // together
    parts, own_dots, own_mixed = pl.pallas_call(
        functools.partial(adjoint_kernel, owned),
        out_shape=(
            jax.ShapeDtypeStruct((batch - 1, channels + DOT_ROWS, span), jnp.bfloat16),
            jax.ShapeDtypeStruct((DOT_ROWS, 128), jnp.bfloat16),
            jax.ShapeDtypeStruct((per_sample, WIDE // 128, rows * CG, 128), jnp.float32),
        ),
        in_specs=[smem, smem] + [anywhere] * (2 + pair_count),
        out_specs=(vmem, vmem, vmem),
        scratch_shapes=[
            pltpu.VMEM((tiles, groups, width), jnp.bfloat16),
            pltpu.VMEM((batch - 1, channels, span), jnp.bfloat16),
            pltpu.VMEM((tiles, groups, width), jnp.bfloat16),
            pltpu.VMEM((rows, width), jnp.float32),
            pltpu.VMEM((WIDE // 128, rows * CG, 128), jnp.float32),
            pltpu.VMEM((PIX // 128, rows * ROW, 128), jnp.float32),
            pltpu.VMEM((samples * per_tile * top_count * groups, 128), jnp.float32),
            pltpu.SemaphoreType.DMA((tiles,)),
            pltpu.SemaphoreType.DMA((2,)),
        ],
        compiler_params=params,
        cost_estimate=pl.CostEstimate(flops=COST, bytes_accessed=1, transcendentals=0),
        name="adjoint",
    )(routes_t, logits_t, wire, got, *pairs)

    own_part = pl.pallas_call(
        own_adjoint_kernel,
        out_shape=jax.ShapeDtypeStruct((channels, span), jnp.bfloat16),
        in_specs=[vmem, vmem],
        out_specs=vmem,
        scratch_shapes=[pltpu.VMEM((PIX // 128, rows * ROW, 128), jnp.float32)],
        compiler_params=params,
        cost_estimate=pl.CostEstimate(flops=COST // 20, bytes_accessed=1, transcendentals=0),
        name="own_adjoint",
    )(own_mixed, cotangent)

    late_routes, late_logits, _ = lax.optimization_barrier((routes_t, logits_t, own_dots))
    local, gate_table = pl.pallas_call(
        functools.partial(tables_kernel, owned, per_tile),
        out_shape=(
            jax.ShapeDtypeStruct((tiles,), jnp.int32),
            jax.ShapeDtypeStruct((tiles, groups, 128), jnp.float32),
        ),
        in_specs=[smem, smem],
        out_specs=(smem, vmem),
        compiler_params=params,
        name="tables",
    )(late_routes, late_logits)

    arrived = exchange([parts[step] for step in range(batch - 1)])
    d_inputs = jnp.zeros(inputs.shape, jnp.bfloat16)
    dots = own_dots[0].astype(jnp.float32)
    for step, part in enumerate([own_part] + arrived):
        block = lax.rem(mine - step + batch, batch)
        d_inputs = lax.dynamic_update_slice(
            d_inputs, part[None, :channels], (0, block * channels, 0)
        )
        if step:
            dots += part[channels, :128].astype(jnp.float32)
    dots = dots[:tiles].reshape(samples, per_tile, top_count)
    gates = jax.nn.sigmoid(
        lax.dynamic_slice_in_dim(late_logits, lax.axis_index("grid") * per_tile, per_tile, 2)
    ).transpose(0, 2, 1)
    gate_grad = gates * (1.0 - gates) * dots / SIDE

    d_weights = pl.pallas_call(
        sum_kernel,
        out_shape=jax.ShapeDtypeStruct(weights.shape, jnp.float32),
        in_specs=[smem, vmem, vmem],
        out_specs=hbm,
        scratch_shapes=[
            pltpu.VMEM(weights.shape, jnp.float32),
            pltpu.SemaphoreType.DMA((SUM_CHUNKS,)),
        ],
        compiler_params=params,
        name="weight_sum",
    )(local, gate_table, grads_back)
    return (d_inputs, d_weights, gate_grad)


def solution(mesh):
    placed = (
        P("batch", None, "grid"),
        P("batch", None, "grid"),
        P("grid", "batch", None),
        P(),
        P(),
    )
    return jax.shard_map(
        per_device,
        mesh=mesh,
        in_specs=placed,
        out_specs=(P("batch", None, "grid"), P("grid", "batch", None), P(None, "grid", None)),
        check_vma=False,
    )
```
